128 devices in a mesh: group: 32 (over x, z, core), shard: 4 (over y).
Axes of the slice: x: 4, y: 4, z: 4, core: 2. Of those that a mesh axis runs over, the one named last changes fastest.
Arguments:
- tokens: bfloat16 [32768, 1024], P(('group', 'shard')), may hold values from -6 to 6
- doc_lengths: int32 [128, 4], P(('group', 'shard')), may hold values from 1 to 128, 256 in all within a row
- cotangent: bfloat16 [32768, 1024], P(('group', 'shard')), may hold values from -6 to 6
- in_weight: float32 [1024, 3072], P(('group', 'shard')), may hold values from -0.1875 to 0.1875
- in_first: float32 [1024, 3072], P(('group', 'shard')), may hold values from -0.00015258789 to 0.00015258789
- in_second: float32 [1024, 3072], P(('group', 'shard')), may hold values from 1.6344143e-09 to 1.0896095e-08
- out_weight: float32 [1024, 1024], P(('group', 'shard')), may hold values from -0.1875 to 0.1875
- out_first: float32 [1024, 1024], P(('group', 'shard')), may hold values from -0.00015258789 to 0.00015258789
- out_second: float32 [1024, 1024], P(('group', 'shard')), may hold values from 1.6344143e-09 to 1.0896095e-08
- ffn_weight: float32 [1024, 9216], P(('group', 'shard')), may hold values from -0.1875 to 0.1875
- ffn_first: float32 [1024, 9216], P(('group', 'shard')), may hold values from -0.00015258789 to 0.00015258789
- ffn_second: float32 [1024, 9216], P(('group', 'shard')), may hold values from 1.6344143e-09 to 1.0896095e-08
- down_weight: float32 [4608, 1024], P(('group', 'shard')), may hold values from -0.09375 to 0.09375
- down_first: float32 [4608, 1024], P(('group', 'shard')), may hold values from -0.00015258789 to 0.00015258789
- down_second: float32 [4608, 1024], P(('group', 'shard')), may hold values from 1.6344143e-09 to 1.0896095e-08
- conv_weight: float32 [3, 1024], P(None, ('group', 'shard')), may hold values from -3.5 to 3.5
- conv_first: float32 [3, 1024], P(None, ('group', 'shard')), may hold values from -0.00048828125 to 0.00048828125
- conv_second: float32 [3, 1024], P(None, ('group', 'shard')), may hold values from 1.4709728e-08 to 9.806485e-08
- gains: float32 [2, 1024], P(None, ('group', 'shard')), may hold values from 0.3 to 3.3, as said below
- gains_first: float32 [2, 1024], P(None, ('group', 'shard')), may hold values from -0.00048828125 to 0.00048828125
- gains_second: float32 [2, 1024], P(None, ('group', 'shard')), may hold values from 1.4709728e-08 to 9.806485e-08
Outputs:
- output: bfloat16 [32768, 1024], P(('group', 'shard'))
- tokens_grad: float32 [32768, 1024], P(('group', 'shard'))
- grad_norm: float32 [], replicated
- new_in_weight: float32 [1024, 3072], P(('group', 'shard'))
- new_in_first: float32 [1024, 3072], P(('group', 'shard'))
- new_in_second: float32 [1024, 3072], P(('group', 'shard'))
- new_out_weight: float32 [1024, 1024], P(('group', 'shard'))
- new_out_first: float32 [1024, 1024], P(('group', 'shard'))
- new_out_second: float32 [1024, 1024], P(('group', 'shard'))
- new_ffn_weight: float32 [1024, 9216], P(('group', 'shard'))
- new_ffn_first: float32 [1024, 9216], P(('group', 'shard'))
- new_ffn_second: float32 [1024, 9216], P(('group', 'shard'))
- new_down_weight: float32 [4608, 1024], P(('group', 'shard'))
- new_down_first: float32 [4608, 1024], P(('group', 'shard'))
- new_down_second: float32 [4608, 1024], P(('group', 'shard'))
- new_conv_weight: float32 [3, 1024], P(None, ('group', 'shard'))
- new_conv_first: float32 [3, 1024], P(None, ('group', 'shard'))
- new_conv_second: float32 [3, 1024], P(None, ('group', 'shard'))
- new_gains: float32 [2, 1024], P(None, ('group', 'shard'))
- new_gains_first: float32 [2, 1024], P(None, ('group', 'shard'))
- new_gains_second: float32 [2, 1024], P(None, ('group', 'shard'))
The draws below stay inside these ranges and needn't reach their ends.
Inputs may be any that keep to these rules, and one draw needn't show every extreme that they name: `doc_lengths`: each row holds the lengths of 4 documents that fill one sequence of 256 tokens; the largest is exactly 128. Positive gains.
All inputs are finite; a program needn't handle non-finite values.
Results may differ from the reference program's by a relative error of at most 0.022.
Values may be sent and summed in bfloat16 or wider, within the bound.
No kernel may reach another device: no remote copies, remote signals or barrier semaphores. Data moves between devices by JAX's collectives and lax.ppermute only.
A program may use at most 256 MiB of HBM per device.

```python
import math
import jax
import jax.numpy as jnp
import numpy as np
from jax import lax

D = 1024
FF = 4608
TOK_DEV = 256
DOCS = 4
STEP = 10
SEQS = 128
TOKENS = 32768
PARAMS = 18355200


def draw_gains(key, part):
    key = jax.random.fold_in(key, 3)
    place = jnp.arange(D, dtype=jnp.float32) / (D - 1)
    base = 0.6 * 3.0 ** place
    jitter = jax.random.uniform(key, (2, D), jnp.float32, 0.8, 1.25)
    return base[None, :] * jitter


def level_of(key, extent, pieces, low, high):
    def one(dim, shards_of):
        draws = jax.random.uniform(jax.random.fold_in(jax.random.fold_in(key, 6), dim), (shards_of,), jnp.float32, low / len(pieces), high / len(pieces))
        return jnp.repeat(jnp.exp(draws), extent[dim] // shards_of).reshape((-1,) + (1,) * (len(extent) - dim - 1))

    loudness = one(*pieces[0])
    for cut in pieces[1:]:
        loudness = loudness * one(*cut)
    return loudness


def profile(number_of, total, bound, skew):
    portions = [(1 << 20) // math.isqrt(standing ** skew) + 1 for standing in range(2, number_of + 1)]
    rest, counts = total - bound - (number_of - 1), [1] * (number_of - 1)
    while rest > 0:
        candidates = [i for i in range(number_of - 1) if counts[i] < bound]
        mass, remaining = sum([portions[i] for i in candidates]), rest
        for i in candidates:
            extra = min(bound - counts[i], max(1, remaining * portions[i] // mass), rest)
            counts[i] = counts[i] + extra
            rest = rest - extra
    return np.array([bound] + counts)


def ragged_sizes(own_key, count, total, reach, skew):
    if count == 2:
        one = jax.random.randint(own_key, (), max(1, total - reach), min(reach, total - 1) + 1)
        return jnp.stack([one, total - one])
    sizes = jnp.asarray(profile(count, total, reach, skew), jnp.int32)
    couples = (count - 1) // 2
    giver, receiver = sizes[1:1 + 2 * couples:2], sizes[2:2 + 2 * couples:2]
    slack = jnp.minimum(giver - 1, reach - receiver)
    shifted = jax.random.randint(jax.random.fold_in(own_key, 1), (couples,), 0, 1 << 20) % (slack + 1)
    sizes = sizes.at[1:1 + 2 * couples:2].set(giver - shifted).at[2:2 + 2 * couples:2].set(receiver + shifted)
    return sizes[jax.random.permutation(jax.random.fold_in(own_key, 2), count)]


def gaussian(stream_key, extent, scale, most, pieces=(), kind=jnp.bfloat16):
    gain = level_of(stream_key, extent, pieces, -0.22, 0.18) if pieces else 1.0
    entries = jax.random.normal(stream_key, extent, jnp.float32) * scale * gain
    return jnp.minimum(jnp.maximum(entries, -most), most).astype(kind)


def setup_inputs(seed: int = 0) -> dict:
    arg_keys = jax.random.split(jax.random.key(seed), 22)
    tokens = gaussian(arg_keys[0], (TOKENS, D), 1.0, 6.0, ((0, 128),))
    doc_lengths = jax.vmap(lambda own: ragged_sizes(own, DOCS, TOK_DEV, TOK_DEV // 2, 1))(jax.random.split(arg_keys[1], SEQS)).reshape((SEQS, DOCS)).astype(jnp.int32)
    cotangent = gaussian(arg_keys[2], (TOKENS, D), 1.0, 6.0, ((0, 128),))
    in_weight = gaussian(arg_keys[3], (D, 3 * D), D ** -0.5, 0.1875, ((0, 128),), jnp.float32)
    in_first = gaussian(arg_keys[4], (D, 3 * D), (0.11 / PARAMS ** 0.5), 0.00015258789, ((0, 128),), jnp.float32)
    in_second = jnp.clip(jnp.exp(math.log(1.0896094693180203e-08) - 1.89712 * jax.random.uniform(arg_keys[5], (D, 3 * D), jnp.float32) ** level_of(arg_keys[5], (D, 3 * D), ((0, 128),), -0.2, 0.2)), 1.6344142705904119e-09, 1.0896094693180203e-08)
    out_weight = gaussian(arg_keys[6], (D, D), D ** -0.5, 0.1875, ((0, 128),), jnp.float32)
    out_first = gaussian(arg_keys[7], (D, D), (0.11 / PARAMS ** 0.5), 0.00015258789, ((0, 128),), jnp.float32)
    out_second = jnp.clip(jnp.exp(math.log(1.0896094693180203e-08) - 1.89712 * jax.random.uniform(arg_keys[8], (D, D), jnp.float32) ** level_of(arg_keys[8], (D, D), ((0, 128),), -0.2, 0.2)), 1.6344142705904119e-09, 1.0896094693180203e-08)
    ffn_weight = gaussian(arg_keys[9], (D, 2 * FF), D ** -0.5, 0.1875, ((0, 128),), jnp.float32)
    ffn_first = gaussian(arg_keys[10], (D, 2 * FF), (0.11 / PARAMS ** 0.5), 0.00015258789, ((0, 128),), jnp.float32)
    ffn_second = jnp.clip(jnp.exp(math.log(1.0896094693180203e-08) - 1.89712 * jax.random.uniform(arg_keys[11], (D, 2 * FF), jnp.float32) ** level_of(arg_keys[11], (D, 2 * FF), ((0, 128),), -0.2, 0.2)), 1.6344142705904119e-09, 1.0896094693180203e-08)
    down_weight = gaussian(arg_keys[12], (FF, D), FF ** -0.5, 0.09375, ((0, 128),), jnp.float32)
    down_first = gaussian(arg_keys[13], (FF, D), (0.11 / PARAMS ** 0.5), 0.00015258789, ((0, 128),), jnp.float32)
    down_second = jnp.clip(jnp.exp(math.log(1.0896094693180203e-08) - 1.89712 * jax.random.uniform(arg_keys[14], (FF, D), jnp.float32) ** level_of(arg_keys[14], (FF, D), ((0, 128),), -0.2, 0.2)), 1.6344142705904119e-09, 1.0896094693180203e-08)
    conv_weight = gaussian(arg_keys[15], (3, D), 3 ** -0.5, 3.5, ((1, 128),), jnp.float32)
    conv_first = gaussian(arg_keys[16], (3, D), (0.33 / PARAMS ** 0.5), 0.00048828125, ((1, 128),), jnp.float32)
    conv_second = jnp.clip(jnp.exp(math.log(9.806485223862182e-08) - 1.89712 * jax.random.uniform(arg_keys[17], (3, D), jnp.float32) ** level_of(arg_keys[17], (3, D), ((1, 128),), -0.2, 0.2)), 1.470972765815759e-08, 9.806485223862182e-08)
    gains = draw_gains(jax.random.fold_in(arg_keys[21], 71), 0)
    gains_first = gaussian(arg_keys[19], (2, D), (0.33 / PARAMS ** 0.5), 0.00048828125, ((1, 128),), jnp.float32)
    gains_second = jnp.clip(jnp.exp(math.log(9.806485223862182e-08) - 1.89712 * jax.random.uniform(arg_keys[20], (2, D), jnp.float32) ** level_of(arg_keys[20], (2, D), ((1, 128),), -0.2, 0.2)), 1.470972765815759e-08, 9.806485223862182e-08)
    return {"tokens": tokens, "doc_lengths": doc_lengths, "cotangent": cotangent, "in_weight": in_weight, "in_first": in_first, "in_second": in_second, "out_weight": out_weight, "out_first": out_first, "out_second": out_second, "ffn_weight": ffn_weight, "ffn_first": ffn_first, "ffn_second": ffn_second, "down_weight": down_weight, "down_first": down_first, "down_second": down_second, "conv_weight": conv_weight, "conv_first": conv_first, "conv_second": conv_second, "gains": gains, "gains_first": gains_first, "gains_second": gains_second}


eps_norm = 1e-05
beta_one = 0.9
beta_two = 0.95
adam_eps = 1e-08
clip_level = 1.0
rate_matrix = 0.03
rate_vector = 0.5
decay_matrix = 0.1

@jax.custom_vjp
def low(v):
    return lax.optimization_barrier(v.astype(jnp.bfloat16)).astype(jnp.float32)

@jax.custom_vjp
def low_back(v):
    return v

def low_keep(v):
    return (low(v), None)

def low_pass(kept, grad):
    return (grad,)

def back_keep(v):
    return (v, None)

def back_low(kept, grad):
    return (low(grad),)
low.defvjp(low_keep, low_pass)
low_back.defvjp(back_keep, back_low)

def matmul(left, right):
    return jnp.dot(left, right, precision=lax.Precision.HIGHEST, preferred_element_type=jnp.float32)

def delay_rows(values, offset):
    if offset == 0:
        return values
    return jnp.concatenate([jnp.zeros_like(values[:, :offset]), values[:, :-offset]], axis=1)

def tap_masks(lengths, row_count):
    lengths = lengths.astype(jnp.int32)
    ends = jnp.cumsum(lengths, axis=1).astype(jnp.int32)
    starts = ends - lengths
    places = jnp.arange(row_count, dtype=jnp.int32)
    begin = lax.optimization_barrier(jnp.max(jnp.where(starts[:, None, :] <= places[None, :, None], starts[:, None, :], 0), axis=2))
    return [(places[None, :] - offset >= begin).astype(jnp.float32)[:, :, None] for offset in range(3)]

def forward(activations, lengths, in_matrix, out_matrix, ffn_matrix, down_matrix, conv_taps, norm_gains):
    count = lengths.shape[0]
    in_matrix = low(in_matrix)
    out_matrix = low(out_matrix)
    ffn_matrix = low(ffn_matrix)
    down_matrix = low(down_matrix)
    conv_taps = low(conv_taps)
    norm_gains = low(norm_gains)
    inverse_one = lax.rsqrt(lax.optimization_barrier(jnp.mean(activations * activations, axis=1, keepdims=True)) + eps_norm)
    normed_one = low(activations * inverse_one * norm_gains[0])
    projected = low_back(matmul(normed_one, in_matrix))
    b_part = projected[:, :D]
    c_part = projected[:, D:2 * D]
    v_part = projected[:, 2 * D:]
    mixed_in = (b_part * v_part).reshape(count, TOK_DEV, D)
    masks = tap_masks(lengths, TOK_DEV)
    conv_out = jnp.zeros_like(mixed_in)
    for offset in range(3):
        conv_out = conv_out + conv_taps[offset] * delay_rows(mixed_in, offset) * masks[offset]
    conv_out = conv_out.reshape(count * TOK_DEV, D)
    gated = low(c_part * conv_out)
    branch = low_back(matmul(gated, out_matrix))
    middle = activations + branch
    inverse_two = lax.rsqrt(lax.optimization_barrier(jnp.mean(middle * middle, axis=1, keepdims=True)) + eps_norm)
    normed_two = low(middle * inverse_two * norm_gains[1])
    both_parts = low_back(matmul(normed_two, ffn_matrix))
    gate_pre = both_parts[:, :FF]
    up_pre = both_parts[:, FF:]
    product = low(jax.nn.silu(gate_pre) * up_pre)
    return middle + matmul(product, down_matrix)

def adam_step(weight, first, second, grad, rate, decay):
    first = beta_one * first + (1.0 - beta_one) * grad
    second = beta_two * second + (1.0 - beta_two) * grad * grad
    mean_hat = first / (1.0 - beta_one ** STEP)
    var_hat = second / (1.0 - beta_two ** STEP)
    weight = weight - rate * (mean_hat / (jnp.sqrt(var_hat) + adam_eps) + decay * weight)
    return (weight, first, second)

def reference(tokens, doc_lengths, cotangent, in_weight, in_first, in_second, out_weight, out_first, out_second, ffn_weight, ffn_first, ffn_second, down_weight, down_first, down_second, conv_weight, conv_first, conv_second, gains, gains_first, gains_second):
    weights = (in_weight, out_weight, ffn_weight, down_weight, conv_weight, gains)
    per_block = max(1, min(SEQS, 4096 // TOK_DEV))
    blocks = SEQS // per_block
    inputs = tokens.astype(jnp.float32).reshape(blocks, per_block * TOK_DEV, D)
    cotangents = cotangent.astype(jnp.float32).reshape(blocks, per_block * TOK_DEV, D)
    lengths_all = doc_lengths.reshape(blocks, per_block, DOCS)

    def block_step(totals, item):
        inputs_block, lengths_block, cot_block = item

        def closed(values, *params):
            return forward(values, lengths_block, *params)
        result, pullback = jax.vjp(closed, inputs_block, *weights)
        grads = pullback(cot_block)
        totals = tuple((total + grad for total, grad in zip(totals, grads[1:])))
        return (totals, (result.astype(jnp.bfloat16), grads[0]))
    zeros_init = tuple((jnp.zeros(weight.shape, jnp.float32) for weight in weights))
    totals, (outputs, input_grads) = lax.scan(block_step, zeros_init, (inputs, lengths_all, cotangents))
    output = outputs.reshape(TOKENS, D)
    tokens_grad = input_grads.reshape(TOKENS, D)
    squares = jnp.float32(0.0)
    for grad in totals:
        squares = squares + jnp.sum(grad * grad)
    grad_norm = jnp.sqrt(squares)
    factor = jnp.minimum(1.0, clip_level / grad_norm)
    states = ((in_weight, in_first, in_second), (out_weight, out_first, out_second), (ffn_weight, ffn_first, ffn_second), (down_weight, down_first, down_second), (conv_weight, conv_first, conv_second), (gains, gains_first, gains_second))
    results = []
    for index in range(6):
        rate = rate_matrix if index < 4 else rate_vector
        decay = decay_matrix if index < 4 else 0.0
        weight, first, second = states[index]
        results.extend(adam_step(weight, first, second, totals[index] * factor, rate, decay))
    return (output, tokens_grad, grad_norm, results[0], results[1], results[2], results[3], results[4], results[5], results[6], results[7], results[8], results[9], results[10], results[11], results[12], results[13], results[14], results[15], results[16], results[17])
```

```python
import jax
import jax.numpy as jnp
from jax import lax
from jax.sharding import Mesh
from jax.sharding import PartitionSpec as P

D = 1024
FF = 4608
STEP = 10
TOK = 256
CH = 512
HID = 2304


eps_norm = 1e-05
beta_one = 0.9
beta_two = 0.95
adam_eps = 1e-08
clip_level = 1.0
rate_matrix = 0.03
rate_vector = 0.5
decay_matrix = 0.1

BF = jnp.bfloat16
F32 = jnp.float32
AXES = ("x", "z", "core", "y")


def dot(left, right):
    return jnp.dot(left, right, preferred_element_type=F32)


def dot_tn(left, right):
    return lax.dot_general(left, right, (((0,), (0,)), ((), ())), preferred_element_type=F32)


def dot_nt(left, right):
    return lax.dot_general(left, right, (((1,), (1,)), ((), ())), preferred_element_type=F32)


def ring_pairs(axis):
    pairs = []
    for place in range(4):
        for core in range(2):
            target = (place + (1 if core == 0 else -1)) % 4
            if axis == "y":
                pairs.append((core * 4 + place, core * 4 + target))
            else:
                pairs.append((place * 2 + core, target * 2 + core))
    return pairs


def hop(value, axis):
    names = ("core", "y") if axis == "y" else (axis, "core")
    return lax.ppermute(value, names, ring_pairs(axis))


def swap(value):
    return lax.ppermute(value, "core", [(0, 1), (1, 0)])


def place_back(axis, steps):
    core = lax.axis_index("core")
    sign = 1 - 2 * core
    return lax.rem(lax.axis_index(axis) - steps * sign + 8, 4)


def gather_ring(block, axis):
    stacked = jnp.zeros((4,) + block.shape, block.dtype)
    for step in range(4):
        if step:
            block = hop(block, axis)
        index = place_back(axis, step)
        stacked = lax.dynamic_update_slice(stacked, block[None], (index,) + (0,) * block.ndim)
    return stacked


def scatter_ring(blocks, axis, dim):
    def own(step):
        return lax.dynamic_index_in_dim(blocks, place_back(axis, step), dim, keepdims=False)

    moving = own(1)
    for step in (2, 3, 4):
        arrived = hop(moving, axis)
        moving = (arrived.astype(F32) + own(step % 4).astype(F32)).astype(BF)
    return moving


def sum_all(value, names):
    for name in names:
        if name == "core":
            value = value + swap(value)
        else:
            others = [
                lax.ppermute(value, name, [(i, (i + shift) % 4) for i in range(4)])
                for shift in (1, 2, 3)
            ]
            value = (value + others[1]) + (others[0] + others[2])
    return value


def split_cols(shard, groups, width):
    rows = shard.shape[0]
    parts = shard.reshape(rows, groups, 16, 2, width)
    return [parts[:, :, :, core, :].reshape(rows, groups * 16 * width) for core in range(2)]


def join_cols(halves, groups, width):
    rows = halves[0].shape[0]
    parts = [half.reshape(rows, groups, 16, 1, width) for half in halves]
    return jnp.concatenate(parts, axis=3).reshape(rows, groups * 32 * width)


def pick(core, zero, one):
    return jnp.where(core == 0, zero, one)


def delay_rows(values, offset):
    if offset == 0:
        return values
    return jnp.concatenate([jnp.zeros_like(values[:, :offset]), values[:, :-offset]], axis=1)


def advance_rows(values, offset):
    if offset == 0:
        return values
    return jnp.concatenate([values[:, offset:], jnp.zeros_like(values[:, :offset])], axis=1)


def tap_masks(lengths):
    ends = jnp.cumsum(lengths, axis=1)
    starts = ends - lengths
    places = jnp.arange(TOK, dtype=jnp.int32)
    begin = jnp.max(
        jnp.where(starts[:, None, :] <= places[None, :, None], starts[:, None, :], 0), axis=2
    )
    return [(places[None, :] - offset >= begin).astype(F32)[:, :, None] for offset in range(3)]


def adam_step(weight, first, second, grad, rate, decay):
    first = beta_one * first + (1.0 - beta_one) * grad
    second = beta_two * second + (1.0 - beta_two) * grad * grad
    mean_hat = first / (1.0 - beta_one**STEP)
    var_hat = second / (1.0 - beta_two**STEP)
    weight = weight - rate * (mean_hat / (jnp.sqrt(var_hat) + adam_eps) + decay * weight)
    return (weight, first, second)


def gather_weights(core, in_weight, out_weight, ffn_weight, down_weight, conv_weight, gains):
    in_halves = split_cols(in_weight.astype(BF), 3, 32)
    ffn_halves = split_cols(ffn_weight.astype(BF), 2, 144)
    gains_low = gains.astype(BF)
    keep = jnp.concatenate([pick(core, *in_halves), pick(core, *ffn_halves)], axis=1)
    send = jnp.concatenate([pick(core, *in_halves[::-1]), pick(core, *ffn_halves[::-1])], axis=1)
    came = swap(send)
    gains_came = swap(gains_low)
    rows = (pick(core, keep, came), pick(core, came, keep))
    gain_rows = (pick(core, gains_low, gains_came), pick(core, gains_came, gains_low))
    small = jnp.concatenate(
        [conv_weight.astype(BF), gain_rows[0], gain_rows[1], jnp.zeros((1, 8), BF)], axis=0
    )
    small = jnp.pad(small, ((0, 0), (0, 120)))
    out_rows = out_weight.astype(BF)

    def in_part(index):
        return [row[:, index * CH : (index + 1) * CH] for row in rows]

    def ffn_part(index):
        return [row[:, 3 * CH + index * HID : 3 * CH + (index + 1) * HID] for row in rows]

    conv_a = jnp.concatenate(in_part(0) + [out_rows[:, :384]], axis=1)
    conv_b = jnp.concatenate(in_part(1) + [out_rows[:, 384:768]], axis=1)
    conv_c = jnp.concatenate(in_part(2) + [out_rows[:, 768:], small], axis=1)
    gate = jnp.concatenate(ffn_part(0), axis=1)
    up = jnp.concatenate(ffn_part(1), axis=1)
    conv_a = gather_ring(gather_ring(gather_ring(conv_a, "y"), "z"), "x")
    conv_b = gather_ring(gather_ring(gather_ring(conv_b, "x"), "y"), "z")
    conv_c = gather_ring(gather_ring(gather_ring(conv_c, "z"), "x"), "y")
    conv_a = conv_a.transpose(0, 1, 2, 3, 4)
    conv_b = conv_b.transpose(2, 0, 1, 3, 4)
    conv_c = conv_c.transpose(1, 2, 0, 3, 4)

    def feature_rows(value, width):
        split = value.reshape(4, 4, 4, 8, 2, width).transpose(0, 1, 4, 2, 3, 5)
        return split.reshape(D, width)

    in_full = jnp.concatenate(
        [feature_rows(conv[..., : 2 * CH], CH) for conv in (conv_a, conv_b, conv_c)], axis=1
    )
    out_full = jnp.concatenate(
        [conv_a[..., 1024:], conv_b[..., 1024:], conv_c[..., 1024:1280]], axis=-1
    ).reshape(CH, D)
    small = conv_c[..., 1280:1288].astype(F32)
    taps = small[:, :, :, 0:3].transpose(3, 0, 1, 2, 4).reshape(3, CH)
    gain_full = small[:, :, :, 3:7].reshape(4, 4, 4, 2, 2, 8)
    gain_full = gain_full.transpose(4, 0, 1, 3, 2, 5).reshape(2, D)

    gate = gather_ring(gather_ring(gather_ring(gate, "x"), "y"), "z")
    up = gather_ring(gather_ring(gather_ring(up, "z"), "x"), "y")
    down = gather_ring(down_weight.astype(BF), "y").reshape(144, D)
    down_full = gather_ring(gather_ring(down, "z"), "x").reshape(HID, D)
    gate_full = feature_rows(gate.transpose(2, 0, 1, 3, 4), HID)
    up_full = feature_rows(up.transpose(1, 2, 0, 3, 4), HID)
    return in_full, out_full, gate_full, up_full, down_full, taps, gain_full


def rows_by_place(grad):
    return grad.reshape(4, 4, 2, 4, 8, grad.shape[1]).transpose(0, 1, 3, 2, 4, 5)


def scatter_a(blocks):
    return scatter_ring(scatter_ring(scatter_ring(blocks, "x", 0), "z", 0), "y", 0)


def scatter_b(blocks):
    return scatter_ring(scatter_ring(scatter_ring(blocks, "z", 1), "y", 1), "x", 0)


def scatter_c(blocks):
    return scatter_ring(scatter_ring(scatter_ring(blocks, "y", 2), "x", 0), "z", 0)


def shards(
    tokens,
    doc_lengths,
    cotangent,
    in_weight,
    in_first,
    in_second,
    out_weight,
    out_first,
    out_second,
    ffn_weight,
    ffn_first,
    ffn_second,
    down_weight,
    down_first,
    down_second,
    conv_weight,
    conv_first,
    conv_second,
    gains,
    gains_first,
    gains_second,
):
    core = lax.axis_index("core")
    in_full, out_full, gate_full, up_full, down_full, taps, gain_full = gather_weights(
        core, in_weight, out_weight, ffn_weight, down_weight, conv_weight, gains
    )
    other_tokens = swap(tokens)
    other_cot = swap(cotangent)
    other_lengths = swap(doc_lengths)
    values = jnp.concatenate(
        [pick(core, tokens, other_tokens), pick(core, other_tokens, tokens)], axis=0
    ).astype(F32)
    cot = jnp.concatenate([pick(core, cotangent, other_cot), pick(core, other_cot, cotangent)], axis=0)
    lengths = jnp.concatenate(
        [pick(core, doc_lengths, other_lengths), pick(core, other_lengths, doc_lengths)], axis=0
    )
    masks = tap_masks(lengths)
    gain_one = gain_full[0]
    gain_two = gain_full[1]

    def own_rows(value):
        return lax.dynamic_slice_in_dim(value, core * TOK, TOK, 0)

    def other_rows(value):
        return lax.dynamic_slice_in_dim(value, (1 - core) * TOK, TOK, 0)

    inverse_one = lax.rsqrt(jnp.mean(values * values, axis=1, keepdims=True) + eps_norm)
    normed_one = (values * inverse_one * gain_one).astype(BF)
    projected = dot(normed_one, in_full).reshape(2, TOK, 3 * CH)
    b_part = projected[..., :CH]
    c_part = projected[..., CH : 2 * CH]
    v_part = projected[..., 2 * CH :]
    mixed_in = b_part * v_part
    shifted = [delay_rows(mixed_in, offset) * masks[offset] for offset in range(3)]
    conv_out = taps[0] * shifted[0] + taps[1] * shifted[1] + taps[2] * shifted[2]
    gated = (c_part * conv_out).astype(BF).reshape(2 * TOK, CH)
    branch = dot(gated, out_full)
    middle = values + (branch + swap(branch))
    inverse_two = lax.rsqrt(jnp.mean(middle * middle, axis=1, keepdims=True) + eps_norm)
    normed_two = (middle * inverse_two * gain_two).astype(BF)
    gate_pre = dot(normed_two, gate_full)
    up_pre = dot(normed_two, up_full)
    sigmoid_gate = jax.nn.sigmoid(gate_pre)
    silu_gate = gate_pre * sigmoid_gate
    product = (silu_gate * up_pre).astype(BF)
    d_product = dot_nt(cot, down_full)
    d_gate = (d_product * up_pre * sigmoid_gate * (1.0 + gate_pre * (1.0 - sigmoid_gate))).astype(BF)
    d_up = (d_product * silu_gate).astype(BF)
    grad_down = dot_tn(product, cot).astype(BF)
    grad_gate = dot_tn(normed_two, d_gate).astype(BF)
    grad_up = dot_tn(normed_two, d_up).astype(BF)
    owned_down = scatter_a(grad_down.reshape(4, 4, 4, 36, D))
    owned_gate = scatter_b(rows_by_place(grad_gate))
    owned_up = scatter_c(rows_by_place(grad_up))

    ffn_out = dot(product, down_full)
    output = (own_rows(middle) + (own_rows(ffn_out) + swap(other_rows(ffn_out)))).astype(BF)

    d_normed_part = dot_nt(d_gate, gate_full) + dot_nt(d_up, up_full)
    d_normed_two = d_normed_part + swap(d_normed_part)
    grad_gain_two = jnp.sum(d_normed_two * middle * inverse_two, axis=0)
    scaled_two = d_normed_two * gain_two
    d_middle = (
        cot.astype(F32)
        + inverse_two * scaled_two
        - middle * inverse_two**3 * jnp.mean(scaled_two * middle, axis=1, keepdims=True)
    )
    d_middle_low = d_middle.astype(BF)
    grad_out = dot_tn(gated, d_middle_low).astype(BF)
    d_gated = dot_nt(d_middle_low, out_full).reshape(2, TOK, CH)
    d_c_part = d_gated * conv_out
    d_conv = d_gated * c_part
    grad_taps = jnp.stack([jnp.sum(d_conv * shifted[k], axis=(0, 1)) for k in range(3)])
    d_mixed = taps[0] * d_conv
    for offset in (1, 2):
        d_mixed = d_mixed + taps[offset] * advance_rows(d_conv * masks[offset], offset)
    d_proj = (
        jnp.concatenate([d_mixed * v_part, d_c_part, d_mixed * b_part], axis=-1)
        .astype(BF)
        .reshape(2 * TOK, 3 * CH)
    )
    grad_in = dot_tn(normed_one, d_proj).astype(BF)
    d_first_part = dot_nt(d_proj, in_full)
    d_normed_one = own_rows(d_first_part) + swap(other_rows(d_first_part))
    own_values = tokens.astype(F32)
    own_inverse = own_rows(inverse_one)
    grad_gain_one = jnp.sum(d_normed_one * own_values * own_inverse, axis=0)
    scaled_one = d_normed_one * gain_one
    tokens_grad = (
        own_rows(d_middle)
        + own_inverse * scaled_one
        - own_values * own_inverse**3 * jnp.mean(scaled_one * own_values, axis=1, keepdims=True)
    )

    in_places = [rows_by_place(grad_in[:, k * CH : (k + 1) * CH]) for k in range(3)]
    in_places = [part.reshape(4, 4, 4, 8 * 2, CH) for part in in_places]
    out_places = grad_out.reshape(4, 4, 4, 8, D)

    def conv_chain(part, out_part):
        both = part.reshape(4, 4, 4, 2, 8, CH).transpose(0, 1, 2, 4, 3, 5).reshape(4, 4, 4, 8, 2 * CH)
        return jnp.concatenate([both, out_part], axis=-1)

    owned_conv = [
        scatter_a(conv_chain(in_places[0], out_places[..., :384])),
        scatter_b(conv_chain(in_places[1], out_places[..., 384:768])),
        scatter_c(conv_chain(in_places[2], out_places[..., 768:])),
    ]
    gain_one_chip = grad_gain_one + swap(grad_gain_one)
    small = jnp.concatenate(
        [
            grad_taps,
            gain_one_chip.reshape(2, CH),
            grad_gain_two.reshape(2, CH),
            jnp.zeros((1, CH), F32),
        ],
        axis=0,
    )
    small = sum_all(small, ("x", "y", "z"))
    place = (lax.axis_index("x") * 4 + lax.axis_index("z")) * 4 + lax.axis_index("y")
    owned_taps = lax.dynamic_slice(small, (0, place * 8), (3, 8))
    gain_sums = jnp.stack([small[3:5].reshape(D), small[5:7].reshape(D)])
    mine = ((lax.axis_index("x") * 4 + lax.axis_index("z")) * 2 + core) * 4 + lax.axis_index("y")
    owned_gains = lax.dynamic_slice(gain_sums, (0, mine * 8), (2, 8))

    def rows_of(which):
        in_rows = [
            lax.dynamic_slice_in_dim(conv[:, : 2 * CH], which * CH, CH, 1) for conv in owned_conv
        ]
        ffn_rows = [
            lax.dynamic_index_in_dim(part, which, 0, keepdims=False)
            for part in (owned_gate, owned_up)
        ]
        return jnp.concatenate(in_rows + ffn_rows, axis=1)

    held = rows_of(core)
    came = swap(rows_of(1 - core))
    halves = (pick(core, held, came).astype(F32), pick(core, came, held).astype(F32))
    owned_in = join_cols([half[:, : 3 * CH] for half in halves], 3, 32)
    owned_ffn = join_cols([half[:, 3 * CH :] for half in halves], 2, 144)
    owned_out = jnp.concatenate([conv[:, 2 * CH :] for conv in owned_conv], axis=1).astype(F32)
    owned = (owned_in, owned_out, owned_ffn, owned_down.astype(F32), owned_taps, owned_gains)

    local_squares = F32(0.0)
    for grad in owned:
        local_squares = local_squares + jnp.sum(grad * grad)
    squares = sum_all(local_squares.reshape(1, 1), ("core", "x", "y", "z"))[0, 0]
    grad_norm = jnp.sqrt(squares)
    factor = jnp.minimum(1.0, clip_level / grad_norm)
    states = (
        (in_weight, in_first, in_second),
        (out_weight, out_first, out_second),
        (ffn_weight, ffn_first, ffn_second),
        (down_weight, down_first, down_second),
        (conv_weight, conv_first, conv_second),
        (gains, gains_first, gains_second),
    )
    results = []
    for index in range(6):
        rate = rate_matrix if index < 4 else rate_vector
        decay = decay_matrix if index < 4 else 0.0
        weight, first, second = states[index]
        results.extend(adam_step(weight, first, second, owned[index] * factor, rate, decay))
    return (output, tokens_grad, grad_norm, *results)


def solution(mesh):
    chips = Mesh(mesh.devices.reshape(4, 4, 2, 4), AXES)
    rows = P(AXES, None)
    columns = P(None, AXES)
    return jax.shard_map(
        shards,
        mesh=chips,
        in_specs=(rows,) * 15 + (columns,) * 6,
        out_specs=(rows, rows, P()) + (rows,) * 12 + (columns,) * 6,
        check_vma=False,
    )
```

```python
import jax
import jax.numpy as jnp
from jax import lax
from jax.sharding import Mesh
from jax.sharding import PartitionSpec as P

D = 1024
FF = 4608
STEP = 10
TOK = 256
CH = 512
HID = 2304


eps_norm = 1e-05
beta_one = 0.9
beta_two = 0.95
adam_eps = 1e-08
clip_level = 1.0
rate_matrix = 0.03
rate_vector = 0.5
decay_matrix = 0.1

BF = jnp.bfloat16
F32 = jnp.float32
AXES = ("x", "z", "core", "y")


def dot(left, right):
    return jnp.dot(left, right, preferred_element_type=F32)


def dot_tn(left, right):
    return lax.dot_general(left, right, (((0,), (0,)), ((), ())), preferred_element_type=F32)


def dot_nt(left, right):
    return lax.dot_general(left, right, (((1,), (1,)), ((), ())), preferred_element_type=F32)


def ring_pairs(axis):
    pairs = []
    for place in range(4):
        for core in range(2):
            target = (place + (1 if core == 0 else -1)) % 4
            if axis == "y":
                pairs.append((core * 4 + place, core * 4 + target))
            else:
                pairs.append((place * 2 + core, target * 2 + core))
    return pairs


def hop(value, axis):
    names = ("core", "y") if axis == "y" else (axis, "core")
    return lax.ppermute(value, names, ring_pairs(axis))


def swap(value):
    return lax.ppermute(value, "core", [(0, 1), (1, 0)])


def place_back(axis, steps):
    core = lax.axis_index("core")
    sign = 1 - 2 * core
    return lax.rem(lax.axis_index(axis) - steps * sign + 8, 4)


def gather_ring(block, axis, dest=None, dim=0, expand=None):
    expand = expand or (lambda value: value[None])
    stacked = jnp.zeros(dest or (4,) + block.shape, block.dtype)
    for step in range(4):
        if step:
            block = hop(block, axis)
        starts = [0] * stacked.ndim
        starts[dim] = place_back(axis, step)
        stacked = lax.dynamic_update_slice(stacked, expand(block), tuple(starts))
    return stacked


def scatter_ring(blocks, axis, dim, gate=None):
    def own(step):
        return lax.dynamic_index_in_dim(blocks, place_back(axis, step), dim, keepdims=False)

    moving = own(1)
    for step in (2, 3, 4):
        arrived = hop(moving, axis)
        if step == 2 and gate is not None:
            arrived = after(arrived, gate)
        moving = (arrived.astype(F32) + own(step % 4).astype(F32)).astype(BF)
    return moving


def sum_all(value):
    spread = jnp.broadcast_to(value, (128, 128))
    return jnp.sum(lax.all_to_all(spread, AXES, 0, 0, tiled=True)[:, 0])


def after(value, *others):
    return lax.optimization_barrier((value, *others))[0]


def split_cols(shard, groups, width):
    rows = shard.shape[0]
    parts = shard.reshape(rows, groups, 16, 2, width)
    return [parts[:, :, :, core, :].reshape(rows, groups * 16 * width) for core in range(2)]


def join_cols(halves, groups, width):
    rows = halves[0].shape[0]
    parts = [half.reshape(rows, groups, 16, 1, width) for half in halves]
    return jnp.concatenate(parts, axis=3).reshape(rows, groups * 32 * width)


def pick(core, zero, one):
    return jnp.where(core == 0, zero, one)


def delay_rows(values, offset):
    if offset == 0:
        return values
    return jnp.concatenate([jnp.zeros_like(values[:, :offset]), values[:, :-offset]], axis=1)


def advance_rows(values, offset):
    if offset == 0:
        return values
    return jnp.concatenate([values[:, offset:], jnp.zeros_like(values[:, :offset])], axis=1)


def tap_masks(lengths):
    ends = jnp.cumsum(lengths, axis=1)
    starts = ends - lengths
    places = jnp.arange(TOK, dtype=jnp.int32)
    begin = jnp.max(
        jnp.where(starts[:, None, :] <= places[None, :, None], starts[:, None, :], 0), axis=2
    )
    return [(places[None, :] - offset >= begin).astype(F32)[:, :, None] for offset in range(3)]


def adam_step(weight, first, second, grad, rate, decay):
    first = beta_one * first + (1.0 - beta_one) * grad
    second = beta_two * second + (1.0 - beta_two) * grad * grad
    mean_hat = first / (1.0 - beta_one**STEP)
    var_hat = second / (1.0 - beta_two**STEP)
    weight = weight - rate * (mean_hat / (jnp.sqrt(var_hat) + adam_eps) + decay * weight)
    return (weight, first, second)


def gather_weights(core, in_weight, out_weight, ffn_weight, down_weight, conv_weight, gains):
    in_halves = split_cols(in_weight.astype(BF), 3, 32)
    ffn_halves = split_cols(ffn_weight.astype(BF), 2, 144)
    gains_low = jnp.pad(gains.astype(BF), ((0, 6), (0, 120)))
    keep = jnp.concatenate([pick(core, *in_halves), pick(core, *ffn_halves), gains_low], axis=1)
    send = jnp.concatenate(
        [pick(core, *in_halves[::-1]), pick(core, *ffn_halves[::-1]), gains_low], axis=1
    )
    came = swap(send)
    rows = (pick(core, keep, came), pick(core, came, keep))
    small = jnp.concatenate(
        [
            jnp.pad(conv_weight.astype(BF), ((0, 0), (0, 120))),
            rows[0][:2, -128:],
            rows[1][:2, -128:],
            jnp.zeros((1, 128), BF),
        ],
        axis=0,
    )
    in_cols = 3 * CH
    conv = jnp.concatenate(
        [rows[0][:, :in_cols], rows[1][:, :in_cols], out_weight.astype(BF), small], axis=1
    )
    conv = lax.all_gather(conv, ("x", "z", "y"), axis=0, tiled=True).reshape(4, 4, 4, 8, -1)
    in_full = jnp.stack([conv[..., :in_cols], conv[..., in_cols : 2 * in_cols]], axis=2)
    in_full = in_full.reshape(D, in_cols)
    out_full = conv[..., 2 * in_cols : 2 * in_cols + D].reshape(CH, D)
    small = conv[..., 2 * in_cols + D : 2 * in_cols + D + 8].astype(F32)
    taps = small[:, :, :, 0:3].transpose(3, 0, 1, 2, 4).reshape(3, CH)
    gain_full = small[:, :, :, 3:7].reshape(4, 4, 4, 2, 2, 8)
    gain_full = gain_full.transpose(4, 0, 1, 3, 2, 5).reshape(2, D)

    gate, up = [
        jnp.stack([row[:, in_cols + k * HID : in_cols + (k + 1) * HID] for row in rows])
        for k in range(2)
    ]
    whole = (4, 4, 2, 4, 8, HID)
    down = gather_ring(down_weight.astype(BF), "y").reshape(144, D)
    gate = gather_ring(gate, "x")
    up = gather_ring(up, "z")
    down = gather_ring(down, "z")
    gate = gather_ring(gate, "y")
    up = gather_ring(up, "x")
    return in_full, out_full, taps, gain_full, (down, gate, up)


def gather_last(blocks, shadow):
    axes = ("x", "z", "y")
    dims = (0, 1, 3)
    places = (
        lambda value: value[None],
        lambda value: value.transpose(1, 2, 0, 3, 4)[:, None],
        lambda value: value[:, :, :, None],
    )
    whole = (4, 4, 2, 4, 8, HID)
    stacked = [jnp.zeros(shape, BF) for shape in ((4, 4, 144, D), whole, whole)]
    for step in range(4):
        if step:
            blocks = [hop(block, axis) for block, axis in zip(blocks, axes)]
        if step == 2:
            *blocks, beside = lax.optimization_barrier((*blocks, shadow()))
        for k in range(3):
            starts = [0] * stacked[k].ndim
            starts[dims[k]] = place_back(axes[k], step)
            stacked[k] = lax.dynamic_update_slice(stacked[k], places[k](blocks[k]), tuple(starts))
    return stacked[0].reshape(HID, D), *[value.reshape(D, HID) for value in stacked[1:]], beside


def shards(
    tokens,
    doc_lengths,
    cotangent,
    in_weight,
    in_first,
    in_second,
    out_weight,
    out_first,
    out_second,
    ffn_weight,
    ffn_first,
    ffn_second,
    down_weight,
    down_first,
    down_second,
    conv_weight,
    conv_first,
    conv_second,
    gains,
    gains_first,
    gains_second,
):
    core = lax.axis_index("core")
    in_full, out_full, taps, gain_full, blocks = gather_weights(
        core, in_weight, out_weight, ffn_weight, down_weight, conv_weight, gains
    )
    other_tokens = swap(tokens)
    other_cot = swap(cotangent)
    other_lengths = swap(doc_lengths)
    values = jnp.concatenate(
        [pick(core, tokens, other_tokens), pick(core, other_tokens, tokens)], axis=0
    ).astype(F32)
    cot = jnp.concatenate([pick(core, cotangent, other_cot), pick(core, other_cot, cotangent)], axis=0)
    lengths = jnp.concatenate(
        [pick(core, doc_lengths, other_lengths), pick(core, other_lengths, doc_lengths)], axis=0
    )
    masks = tap_masks(lengths)
    gain_one = gain_full[0]
    gain_two = gain_full[1]

    def own_rows(value):
        return lax.dynamic_slice_in_dim(value, core * TOK, TOK, 0)

    def other_rows(value):
        return lax.dynamic_slice_in_dim(value, (1 - core) * TOK, TOK, 0)

    inverse_one = lax.rsqrt(jnp.mean(values * values, axis=1, keepdims=True) + eps_norm)
    normed_one = (values * inverse_one * gain_one).astype(BF)
    projected = dot(normed_one, in_full).reshape(2, TOK, 3 * CH)
    b_part = projected[..., :CH]
    c_part = projected[..., CH : 2 * CH]
    v_part = projected[..., 2 * CH :]
    mixed_in = b_part * v_part
    shifted = [delay_rows(mixed_in, offset) * masks[offset] for offset in range(3)]
    conv_out = taps[0] * shifted[0] + taps[1] * shifted[1] + taps[2] * shifted[2]
    gated = (c_part * conv_out).astype(BF).reshape(2 * TOK, CH)
    down_full, gate_full, up_full, branch = gather_last(blocks, lambda: dot(gated, out_full))
    middle = values + (branch + swap(branch))
    inverse_two = lax.rsqrt(jnp.mean(middle * middle, axis=1, keepdims=True) + eps_norm)
    normed_two = (middle * inverse_two * gain_two).astype(BF)
    gate_pre = dot(normed_two, gate_full)
    up_pre = dot(normed_two, up_full)
    sigmoid_gate = jax.nn.sigmoid(gate_pre)
    silu_gate = gate_pre * sigmoid_gate
    product = (silu_gate * up_pre).astype(BF)
    d_product = dot_nt(cot, down_full)
    d_gate = (d_product * up_pre * sigmoid_gate * (1.0 + gate_pre * (1.0 - sigmoid_gate))).astype(BF)
    d_up = (d_product * silu_gate).astype(BF)
    grad_down = dot_tn(product, cot).astype(BF)
    grad_gate = dot_tn(normed_two, d_gate).astype(BF)
    grad_up = dot_tn(normed_two, d_up).astype(BF)
    d_normed_part = dot_nt(d_gate, gate_full) + dot_nt(d_up, up_full)
    d_normed_two = d_normed_part + swap(d_normed_part)
    grad_gain_two = jnp.sum(d_normed_two * middle * inverse_two, axis=0)
    scaled_two = d_normed_two * gain_two
    d_middle = (
        cot.astype(F32)
        + inverse_two * scaled_two
        - middle * inverse_two**3 * jnp.mean(scaled_two * middle, axis=1, keepdims=True)
    )
    d_middle_low = d_middle.astype(BF)
    grad_out = dot_tn(gated, d_middle_low).astype(BF)
    d_gated = dot_nt(d_middle_low, out_full).reshape(2, TOK, CH)
    d_c_part = d_gated * conv_out
    d_conv = d_gated * c_part
    grad_taps = jnp.stack([jnp.sum(d_conv * shifted[k], axis=(0, 1)) for k in range(3)])
    d_mixed = taps[0] * d_conv
    for offset in (1, 2):
        d_mixed = d_mixed + taps[offset] * advance_rows(d_conv * masks[offset], offset)
    d_proj = (
        jnp.concatenate([d_mixed * v_part, d_c_part, d_mixed * b_part], axis=-1)
        .astype(BF)
        .reshape(2 * TOK, 3 * CH)
    )
    grad_in = dot_tn(normed_one, d_proj).astype(BF)
    in_rows = grad_in.reshape(4, 4, 2, 4, 8, 3 * CH)
    out_rows = grad_out.reshape(4, 4, 4, 8, D)
    conv = jnp.concatenate([in_rows[:, :, 0], in_rows[:, :, 1], out_rows], axis=-1)
    conv = conv.reshape(512, 4096)

    part_a = scatter_ring(grad_down.reshape(4, 4, 144, D), "x", 0, conv)
    part_b = scatter_ring(grad_gate.reshape(4, 4, 2, 4, 8, HID), "z", 1, conv)
    part_c = scatter_ring(grad_up.reshape(4, 4, 2, 4, 8, HID), "y", 3, conv)
    summed = lax.psum_scatter(conv, ("x", "z"), scatter_dimension=0, tiled=True)

    ffn_out = dot(after(product, conv), down_full)
    output = (own_rows(middle) + (own_rows(ffn_out) + swap(other_rows(ffn_out)))).astype(BF)
    d_first_part = dot_nt(after(d_proj, conv), in_full)
    d_normed_one = own_rows(d_first_part) + swap(other_rows(d_first_part))
    own_values = tokens.astype(F32)
    own_inverse = own_rows(inverse_one)
    grad_gain_one = jnp.sum(d_normed_one * own_values * own_inverse, axis=0)
    scaled_one = d_normed_one * gain_one
    tokens_grad = (
        own_rows(d_middle)
        + own_inverse * scaled_one
        - own_values * own_inverse**3 * jnp.mean(scaled_one * own_values, axis=1, keepdims=True)
    )

    gain_sums = jnp.stack([grad_gain_one + swap(grad_gain_one), grad_gain_two])
    gain_sums = gain_sums.reshape(2, 16, 2, 32)
    gain_sums = pick(core, gain_sums[:, :, 0], gain_sums[:, :, 1]).reshape(2, CH)
    small = jnp.concatenate([grad_taps, gain_sums, jnp.zeros((3, CH), F32)], axis=0)
    small = small.reshape(8, 64, 8).transpose(1, 0, 2).reshape(64, 64)
    small = lax.all_to_all(small, ("x", "z", "y"), 0, 0, tiled=True)
    owned_small = jnp.sum(small, axis=0).reshape(8, 8)
    owned_taps = owned_small[:3]
    owned_gains = owned_small[3:5]

    part_a = scatter_ring(part_a, "z", 0)
    part_b = scatter_ring(part_b, "y", 2)
    part_c = scatter_ring(part_c, "x", 0)
    owned_down = scatter_ring(part_a.reshape(4, 36, D), "y", 0)
    part_b = scatter_ring(part_b, "x", 0)
    part_c = scatter_ring(part_c, "z", 0)
    conv = scatter_ring(summed.reshape(4, 8, 4096), "y", 0)

    def rows_of(which):
        zero, one = [
            jnp.concatenate(
                [
                    conv[:, place * 3 * CH : (place + 1) * 3 * CH],
                    part_b[place],
                    part_c[place],
                ],
                axis=1,
            )
            for place in range(2)
        ]
        return pick(which, zero, one)

    held = rows_of(core)
    came = swap(rows_of(1 - core))
    halves = (pick(core, held, came).astype(F32), pick(core, came, held).astype(F32))
    owned_in = join_cols([half[:, : 3 * CH] for half in halves], 3, 32)
    owned_ffn = join_cols([half[:, 3 * CH :] for half in halves], 2, 144)
    owned_out = conv[:, 6 * CH : 6 * CH + D].astype(F32)
    owned = (owned_in, owned_out, owned_ffn, owned_down.astype(F32), owned_taps, owned_gains)

    local_squares = F32(0.0)
    for grad in owned:
        local_squares = local_squares + jnp.sum(grad * grad)
    squares = sum_all(local_squares)
    grad_norm = jnp.sqrt(squares)
    factor = jnp.minimum(1.0, clip_level / grad_norm)
    states = (
        (in_weight, in_first, in_second),
        (out_weight, out_first, out_second),
        (ffn_weight, ffn_first, ffn_second),
        (down_weight, down_first, down_second),
        (conv_weight, conv_first, conv_second),
        (gains, gains_first, gains_second),
    )
    results = []
    for index in range(6):
        rate = rate_matrix if index < 4 else rate_vector
        decay = decay_matrix if index < 4 else 0.0
        weight, first, second = states[index]
        results.extend(adam_step(weight, first, second, owned[index] * factor, rate, decay))
    return (output, tokens_grad, grad_norm, *results)


def solution(mesh):
    chips = Mesh(mesh.devices.reshape(4, 4, 2, 4), AXES)
    rows = P(AXES, None)
    columns = P(None, AXES)
    return jax.shard_map(
        shards,
        mesh=chips,
        in_specs=(rows,) * 15 + (columns,) * 6,
        out_specs=(rows, rows, P()) + (rows,) * 12 + (columns,) * 6,
        check_vma=False,
    )
```

```python
import jax
import jax.numpy as jnp
from jax import lax
from jax.experimental import pallas as pl
from jax.experimental.pallas import tpu as pltpu
from jax.sharding import Mesh
from jax.sharding import PartitionSpec as P

D = 1024
FF = 4608
STEP = 10
TOK = 256
CH = 512
HID = 2304


eps_norm = 1e-05
beta_one = 0.9
beta_two = 0.95
adam_eps = 1e-08
clip_level = 1.0
rate_matrix = 0.03
rate_vector = 0.5
decay_matrix = 0.1

BF = jnp.bfloat16
F32 = jnp.float32
AXES = ("x", "z", "core", "y")


def dot(left, right):
    return jnp.dot(left, right, preferred_element_type=F32)


def dot_tn(left, right):
    return lax.dot_general(left, right, (((0,), (0,)), ((), ())), preferred_element_type=F32)


def dot_nt(left, right):
    return lax.dot_general(left, right, (((1,), (1,)), ((), ())), preferred_element_type=F32)


def ring_pairs(axis):
    pairs = []
    for place in range(4):
        for core in range(2):
            target = (place + (1 if core == 0 else -1)) % 4
            if axis == "y":
                pairs.append((core * 4 + place, core * 4 + target))
            else:
                pairs.append((place * 2 + core, target * 2 + core))
    return pairs


def hop(value, axis):
    names = ("core", "y") if axis == "y" else (axis, "core")
    return lax.ppermute(value, names, ring_pairs(axis))


def swap(value):
    return lax.ppermute(value, "core", [(0, 1), (1, 0)])


def place_back(axis, steps):
    core = lax.axis_index("core")
    sign = 1 - 2 * core
    return lax.rem(lax.axis_index(axis) - steps * sign + 8, 4)


def gather_ring(block, axis, dest=None, dim=0, expand=None):
    expand = expand or (lambda value: value[None])
    stacked = jnp.zeros(dest or (4,) + block.shape, block.dtype)
    for step in range(4):
        if step:
            block = hop(block, axis)
        starts = [0] * stacked.ndim
        starts[dim] = place_back(axis, step)
        stacked = lax.dynamic_update_slice(stacked, expand(block), tuple(starts))
    return stacked


FIRST = (1, 3)
SECOND = (3, 1)


def exchange(value, axis, masks):
    names = ("core", "y") if axis == "y" else (axis, "core")
    pairs = []
    for place in range(4):
        for core in range(2):
            target = place ^ masks[core]
            if axis == "y":
                pairs.append((core * 4 + place, core * 4 + target))
            else:
                pairs.append((place * 2 + core, target * 2 + core))
    return lax.ppermute(value, names, pairs)


def spots(axis):
    core = lax.axis_index("core")
    place = lax.axis_index(axis)
    return place, place ^ (3 - 2 * core), place ^ (1 + 2 * core), place ^ 2


def take(blocks, axis, dim):
    return [lax.dynamic_index_in_dim(blocks, spot, dim, keepdims=False) for spot in spots(axis)]


def add(*values):
    total = values[0].astype(F32)
    for value in values[1:]:
        total = total + value.astype(F32)
    return total.astype(BF)


def scatter_start(blocks, axis, dim):
    _, _, first, across = take(blocks, axis, dim)
    return exchange(jnp.stack([first, across]), axis, FIRST)


def scatter_next(blocks, got, axis, dim):
    return add(got[1], take(blocks, axis, dim)[1])


def scatter_end(blocks, got, last, axis, dim):
    return add(got[0], take(blocks, axis, dim)[0], last)


def scatter_ring(blocks, axis, dim):
    got = scatter_start(blocks, axis, dim)
    last = exchange(scatter_next(blocks, got, axis, dim), axis, SECOND)
    return scatter_end(blocks, got, last, axis, dim)


def sum_all(value):
    spread = jnp.broadcast_to(value, (128, 128))
    return jnp.sum(lax.all_to_all(spread, AXES, 0, 0, tiled=True)[:, 0])


def split_cols(shard, groups, width):
    rows = shard.shape[0]
    parts = shard.reshape(rows, groups, 16, 2, width)
    return [parts[:, :, :, core, :].reshape(rows, groups * 16 * width) for core in range(2)]


def join_cols(halves, groups, width):
    rows = halves[0].shape[0]
    parts = [half.reshape(rows, groups, 16, 1, width) for half in halves]
    return jnp.concatenate(parts, axis=3).reshape(rows, groups * 32 * width)


def pick(core, zero, one):
    return jnp.where(core == 0, zero, one)


def delay_rows(values, offset):
    if offset == 0:
        return values
    return jnp.concatenate([jnp.zeros_like(values[:, :offset]), values[:, :-offset]], axis=1)


def advance_rows(values, offset):
    if offset == 0:
        return values
    return jnp.concatenate([values[:, offset:], jnp.zeros_like(values[:, :offset])], axis=1)


def tap_masks(lengths):
    ends = jnp.cumsum(lengths, axis=1)
    starts = ends - lengths
    places = jnp.arange(TOK, dtype=jnp.int32)
    begin = jnp.max(
        jnp.where(starts[:, None, :] <= places[None, :, None], starts[:, None, :], 0), axis=2
    )
    return [(places[None, :] - offset >= begin).astype(F32)[:, :, None] for offset in range(3)]


def adam_step(weight, first, second, grad, rate, decay):
    first = beta_one * first + (1.0 - beta_one) * grad
    second = beta_two * second + (1.0 - beta_two) * grad * grad
    mean_hat = first / (1.0 - beta_one**STEP)
    var_hat = second / (1.0 - beta_two**STEP)
    weight = weight - rate * (mean_hat / (jnp.sqrt(var_hat) + adam_eps) + decay * weight)
    return (weight, first, second)


def gather_weights(core, in_weight, out_weight, ffn_weight, down_weight, conv_weight, gains):
    in_halves = split_cols(in_weight.astype(BF), 3, 32)
    ffn_halves = split_cols(ffn_weight.astype(BF), 2, 144)
    gains_low = jnp.pad(gains.astype(BF), ((0, 6), (0, 120)))
    keep = jnp.concatenate([pick(core, *in_halves), pick(core, *ffn_halves), gains_low], axis=1)
    send = jnp.concatenate(
        [pick(core, *in_halves[::-1]), pick(core, *ffn_halves[::-1]), gains_low], axis=1
    )
    came = swap(send)
    rows = (pick(core, keep, came), pick(core, came, keep))
    small = jnp.concatenate(
        [
            jnp.pad(conv_weight.astype(BF), ((0, 0), (0, 120))),
            rows[0][:2, -128:],
            rows[1][:2, -128:],
            jnp.zeros((1, 128), BF),
        ],
        axis=0,
    )
    in_cols = 3 * CH
    conv = jnp.concatenate(
        [rows[0][:, :in_cols], rows[1][:, :in_cols], out_weight.astype(BF), small], axis=1
    )
    conv = lax.all_gather(conv, ("x", "z", "y"), axis=0, tiled=True).reshape(4, 4, 4, 8, -1)
    in_full = jnp.stack([conv[..., :in_cols], conv[..., in_cols : 2 * in_cols]], axis=2)
    in_full = in_full.reshape(D, in_cols)
    out_full = conv[..., 2 * in_cols : 2 * in_cols + D].reshape(CH, D)
    small = conv[..., 2 * in_cols + D : 2 * in_cols + D + 8].astype(F32)
    taps = small[:, :, :, 0:3].transpose(3, 0, 1, 2, 4).reshape(3, CH)
    gain_full = small[:, :, :, 3:7].reshape(4, 4, 4, 2, 2, 8)
    gain_full = gain_full.transpose(4, 0, 1, 3, 2, 5).reshape(2, D)

    gate, up = [
        jnp.stack([row[:, in_cols + k * HID : in_cols + (k + 1) * HID] for row in rows])
        for k in range(2)
    ]
    whole = (4, 4, 2, 4, 8, HID)
    down = gather_ring(down_weight.astype(BF), "y").reshape(144, D)
    gate = gather_ring(gate, "x")
    up = gather_ring(up, "z")
    down = gather_ring(down, "z")
    gate = gather_ring(gate, "y")
    up = gather_ring(up, "x")
    return in_full, out_full, taps, gain_full, (down, gate, up)


def gather_last(blocks, shadow):
    axes = ("x", "z", "y")
    dims = (0, 1, 3)
    places = (
        lambda value: value[None],
        lambda value: value.transpose(1, 2, 0, 3, 4)[:, None],
        lambda value: value[:, :, :, None],
    )
    whole = (4, 4, 2, 4, 8, HID)
    stacked = [jnp.zeros(shape, BF) for shape in ((4, 4, 144, D), whole, whole)]
    for step in range(4):
        if step:
            blocks = [hop(block, axis) for block, axis in zip(blocks, axes)]
        if step == 3:
            *blocks, beside = lax.optimization_barrier((*blocks, shadow()))
        for k in range(3):
            starts = [0] * stacked[k].ndim
            starts[dims[k]] = place_back(axes[k], step)
            stacked[k] = lax.dynamic_update_slice(stacked[k], places[k](blocks[k]), tuple(starts))
    return stacked[0].reshape(HID, D), *[value.reshape(D, HID) for value in stacked[1:]], beside


TILE = 256


def ffn_kernel(
    normed, cot, gate_w, up_w, down_w, grad_down, grad_gate, grad_up, d_normed, out, normed_t
):
    @pl.when(pl.program_id(0) == 0)
    def _():
        normed_t[...] = normed[...].T
        d_normed[...] = jnp.zeros_like(d_normed)
        out[...] = jnp.zeros_like(out)

    gate_pre = dot(normed[...], gate_w[...])
    up_pre = dot(normed[...], up_w[...])
    d_product = dot_nt(cot[...], down_w[...])
    sigmoid_gate = jax.nn.sigmoid(gate_pre)
    silu_gate = gate_pre * sigmoid_gate
    product = (silu_gate * up_pre).astype(BF)
    d_gate = (d_product * up_pre * sigmoid_gate * (1.0 + gate_pre * (1.0 - sigmoid_gate))).astype(BF)
    d_up = (d_product * silu_gate).astype(BF)
    grad_gate[...] = dot(normed_t[...], d_gate).astype(BF)
    grad_up[...] = dot(normed_t[...], d_up).astype(BF)
    grad_down[...] = dot_tn(product, cot[...]).astype(BF)
    d_normed[...] += dot_nt(d_gate, gate_w[...]) + dot_nt(d_up, up_w[...])
    out[...] += dot(product, down_w[...])


def ffn_block(normed, cot, gate_w, up_w, down_w):
    rows = normed.shape[0]
    fixed = lambda shape: pl.BlockSpec(shape, lambda i: (0, 0))
    wide = pl.BlockSpec((D, TILE), lambda i: (0, i))
    tall = pl.BlockSpec((TILE, D), lambda i: (i, 0))
    return pl.pallas_call(
        ffn_kernel,
        grid=(HID // TILE,),
        in_specs=[fixed((rows, D)), fixed((rows, D)), wide, wide, tall],
        out_specs=[tall, wide, wide, fixed((rows, D)), fixed((rows, D))],
        out_shape=[
            jax.ShapeDtypeStruct((HID, D), BF),
            jax.ShapeDtypeStruct((D, HID), BF),
            jax.ShapeDtypeStruct((D, HID), BF),
            jax.ShapeDtypeStruct((rows, D), F32),
            jax.ShapeDtypeStruct((rows, D), F32),
        ],
        scratch_shapes=[pltpu.VMEM((D, rows), BF)],
        compiler_params=pltpu.CompilerParams(
            dimension_semantics=("arbitrary",), vmem_limit_bytes=48 * 1024 * 1024
        ),
        cost_estimate=pl.CostEstimate(
            flops=18 * rows * D * HID, bytes_accessed=40 * 1024 * 1024, transcendentals=rows * HID
        ),
    )(normed, cot, gate_w, up_w, down_w)


def shards(
    tokens,
    doc_lengths,
    cotangent,
    in_weight,
    in_first,
    in_second,
    out_weight,
    out_first,
    out_second,
    ffn_weight,
    ffn_first,
    ffn_second,
    down_weight,
    down_first,
    down_second,
    conv_weight,
    conv_first,
    conv_second,
    gains,
    gains_first,
    gains_second,
):
    core = lax.axis_index("core")
    in_full, out_full, taps, gain_full, blocks = gather_weights(
        core, in_weight, out_weight, ffn_weight, down_weight, conv_weight, gains
    )
    other_tokens = swap(tokens)
    other_cot = swap(cotangent)
    other_lengths = swap(doc_lengths)
    values = jnp.concatenate(
        [pick(core, tokens, other_tokens), pick(core, other_tokens, tokens)], axis=0
    ).astype(F32)
    cot = jnp.concatenate([pick(core, cotangent, other_cot), pick(core, other_cot, cotangent)], axis=0)
    lengths = jnp.concatenate(
        [pick(core, doc_lengths, other_lengths), pick(core, other_lengths, doc_lengths)], axis=0
    )
    masks = tap_masks(lengths)
    gain_one = gain_full[0]
    gain_two = gain_full[1]

    def own_rows(value):
        return lax.dynamic_slice_in_dim(value, core * TOK, TOK, 0)

    def other_rows(value):
        return lax.dynamic_slice_in_dim(value, (1 - core) * TOK, TOK, 0)

    inverse_one = lax.rsqrt(jnp.mean(values * values, axis=1, keepdims=True) + eps_norm)
    normed_one = (values * inverse_one * gain_one).astype(BF)
    projected = dot(normed_one, in_full).reshape(2, TOK, 3 * CH)
    b_part = projected[..., :CH]
    c_part = projected[..., CH : 2 * CH]
    v_part = projected[..., 2 * CH :]
    mixed_in = b_part * v_part
    shifted = [delay_rows(mixed_in, offset) * masks[offset] for offset in range(3)]
    conv_out = taps[0] * shifted[0] + taps[1] * shifted[1] + taps[2] * shifted[2]
    gated = (c_part * conv_out).astype(BF).reshape(2 * TOK, CH)
    branch = dot(gated, out_full)
    middle = values + (branch + swap(branch))
    inverse_two = lax.rsqrt(jnp.mean(middle * middle, axis=1, keepdims=True) + eps_norm)
    down_full, gate_full, up_full, normed_two = gather_last(
        blocks, lambda: (middle * inverse_two * gain_two).astype(BF)
    )
    grad_down, grad_gate, grad_up, d_normed_part, ffn_out = ffn_block(
        normed_two, cot, gate_full, up_full, down_full
    )
    d_normed_two = d_normed_part + swap(d_normed_part)
    grad_gain_two = jnp.sum(d_normed_two * middle * inverse_two, axis=0)
    scaled_two = d_normed_two * gain_two
    d_middle = (
        cot.astype(F32)
        + inverse_two * scaled_two
        - middle * inverse_two**3 * jnp.mean(scaled_two * middle, axis=1, keepdims=True)
    )
    d_middle_low = d_middle.astype(BF)
    grad_out = dot_tn(gated, d_middle_low).astype(BF)
    d_gated = dot_nt(d_middle_low, out_full).reshape(2, TOK, CH)
    d_c_part = d_gated * conv_out
    d_conv = d_gated * c_part
    grad_taps = jnp.stack([jnp.sum(d_conv * shifted[k], axis=(0, 1)) for k in range(3)])
    d_mixed = taps[0] * d_conv
    for offset in (1, 2):
        d_mixed = d_mixed + taps[offset] * advance_rows(d_conv * masks[offset], offset)
    d_proj = (
        jnp.concatenate([d_mixed * v_part, d_c_part, d_mixed * b_part], axis=-1)
        .astype(BF)
        .reshape(2 * TOK, 3 * CH)
    )
    grad_in = dot_tn(normed_one, d_proj).astype(BF)
    in_rows = grad_in.reshape(4, 4, 2, 4, 8, 3 * CH)
    out_rows = grad_out.reshape(4, 4, 4, 8, D)
    conv = jnp.concatenate([in_rows[:, :, 0], in_rows[:, :, 1], out_rows], axis=-1)
    conv = conv.reshape(512, 4096)

    grads = (
        grad_down.reshape(4, 4, 144, D),
        grad_gate.reshape(4, 4, 2, 4, 8, HID),
        grad_up.reshape(4, 4, 2, 4, 8, HID),
    )
    axes = ("x", "z", "y")
    dims = (0, 1, 3)
    got = [scatter_start(*item) for item in zip(grads, axes, dims)]
    summed = lax.psum_scatter(conv, ("x", "z"), scatter_dimension=0, tiled=True)
    *got, _ = lax.optimization_barrier((*got, conv))
    moving = [scatter_next(*item) for item in zip(grads, got, axes, dims)]
    last = [exchange(value, axis, SECOND) for value, axis in zip(moving, axes)]
    *last, ffn_out = lax.optimization_barrier((*last, ffn_out))
    part_a, part_b, part_c = [scatter_end(*item) for item in zip(grads, got, last, axes, dims)]

    d_first_part = dot_nt(d_proj, in_full)
    d_normed_one = own_rows(d_first_part) + swap(other_rows(d_first_part))
    own_values = tokens.astype(F32)
    own_inverse = own_rows(inverse_one)
    grad_gain_one = jnp.sum(d_normed_one * own_values * own_inverse, axis=0)
    scaled_one = d_normed_one * gain_one
    tokens_grad = (
        own_rows(d_middle)
        + own_inverse * scaled_one
        - own_values * own_inverse**3 * jnp.mean(scaled_one * own_values, axis=1, keepdims=True)
    )
    output = (own_rows(middle) + (own_rows(ffn_out) + swap(other_rows(ffn_out)))).astype(BF)

    gain_sums = jnp.stack([grad_gain_one + swap(grad_gain_one), grad_gain_two])
    gain_sums = gain_sums.reshape(2, 16, 2, 32)
    gain_sums = pick(core, gain_sums[:, :, 0], gain_sums[:, :, 1]).reshape(2, CH)
    small = jnp.concatenate([grad_taps, gain_sums, jnp.zeros((3, CH), F32)], axis=0)
    small = small.reshape(8, 64, 8).transpose(1, 0, 2).reshape(64, 64)
    small = lax.all_to_all(small, ("x", "z", "y"), 0, 0, tiled=True)
    part_a, part_b, part_c, small = lax.optimization_barrier((part_a, part_b, part_c, small))
    owned_small = jnp.sum(small, axis=0).reshape(8, 8)
    owned_taps = owned_small[:3]
    owned_gains = owned_small[3:5]

    part_a = scatter_ring(part_a, "z", 0)
    part_b = scatter_ring(part_b, "y", 2)
    part_c = scatter_ring(part_c, "x", 0)
    part_a, part_b, part_c, summed = lax.optimization_barrier((part_a, part_b, part_c, summed))
    owned_down = scatter_ring(part_a.reshape(4, 36, D), "y", 0)
    part_b = scatter_ring(part_b, "x", 0)
    part_c = scatter_ring(part_c, "z", 0)
    conv = scatter_ring(summed.reshape(4, 8, 4096), "y", 0)

    local_squares = F32(0.0)
    for part in (owned_down, part_b, part_c, conv, owned_small[:5]):
        part = part.astype(F32)
        local_squares = local_squares + jnp.sum(part * part)
    squares = sum_all(local_squares)
    grad_norm = jnp.sqrt(squares)
    factor = jnp.minimum(1.0, clip_level / grad_norm)

    def rows_of(which):
        zero, one = [
            jnp.concatenate(
                [
                    conv[:, place * 3 * CH : (place + 1) * 3 * CH],
                    part_b[place],
                    part_c[place],
                ],
                axis=1,
            )
            for place in range(2)
        ]
        return pick(which, zero, one)

    held = rows_of(core)
    came = swap(rows_of(1 - core))
    halves = (pick(core, held, came).astype(F32), pick(core, came, held).astype(F32))
    owned_in = join_cols([half[:, : 3 * CH] for half in halves], 3, 32)
    owned_ffn = join_cols([half[:, 3 * CH :] for half in halves], 2, 144)
    owned_out = conv[:, 6 * CH : 6 * CH + D].astype(F32)
    owned = (owned_in, owned_out, owned_ffn, owned_down.astype(F32), owned_taps, owned_gains)

    *owned, factor = lax.optimization_barrier((*owned, factor))
    states = (
        (in_weight, in_first, in_second),
        (out_weight, out_first, out_second),
        (ffn_weight, ffn_first, ffn_second),
        (down_weight, down_first, down_second),
        (conv_weight, conv_first, conv_second),
        (gains, gains_first, gains_second),
    )
    results = []
    for index in range(6):
        rate = rate_matrix if index < 4 else rate_vector
        decay = decay_matrix if index < 4 else 0.0
        weight, first, second = states[index]
        results.extend(adam_step(weight, first, second, owned[index] * factor, rate, decay))
    return (output, tokens_grad, grad_norm, *results)


def solution(mesh):
    chips = Mesh(mesh.devices.reshape(4, 4, 2, 4), AXES)
    rows = P(AXES, None)
    columns = P(None, AXES)
    return jax.shard_map(
        shards,
        mesh=chips,
        in_specs=(rows,) * 15 + (columns,) * 6,
        out_specs=(rows, rows, P()) + (rows,) * 12 + (columns,) * 6,
        check_vma=False,
    )
```

```python
import jax
import jax.numpy as jnp
from jax import lax
from jax.experimental import pallas as pl
from jax.experimental.pallas import tpu as pltpu
from jax.sharding import Mesh
from jax.sharding import PartitionSpec as P

D = 1024
FF = 4608
STEP = 10
TOK = 256
CH = 512
HID = 2304


eps_norm = 1e-05
beta_one = 0.9
beta_two = 0.95
adam_eps = 1e-08
clip_level = 1.0
rate_matrix = 0.03
rate_vector = 0.5
decay_matrix = 0.1

BF = jnp.bfloat16
F32 = jnp.float32
AXES = ("x", "z", "core", "y")


def dot(left, right):
    return jnp.dot(left, right, preferred_element_type=F32)


def dot_tn(left, right):
    return lax.dot_general(left, right, (((0,), (0,)), ((), ())), preferred_element_type=F32)


def dot_nt(left, right):
    return lax.dot_general(left, right, (((1,), (1,)), ((), ())), preferred_element_type=F32)


def ring_pairs(axis):
    pairs = []
    for place in range(4):
        for core in range(2):
            target = (place + (1 if core == 0 else -1)) % 4
            if axis == "y":
                pairs.append((core * 4 + place, core * 4 + target))
            else:
                pairs.append((place * 2 + core, target * 2 + core))
    return pairs


def hop(value, axis):
    names = ("core", "y") if axis == "y" else (axis, "core")
    return lax.ppermute(value, names, ring_pairs(axis))


def swap(value):
    return lax.ppermute(value, "core", [(0, 1), (1, 0)])


def place_back(axis, steps):
    core = lax.axis_index("core")
    sign = 1 - 2 * core
    return lax.rem(lax.axis_index(axis) - steps * sign + 8, 4)


def gather_ring(block, axis, dest=None, dim=0, expand=None):
    expand = expand or (lambda value: value[None])
    stacked = jnp.zeros(dest or (4,) + block.shape, block.dtype)
    for step in range(4):
        if step:
            block = hop(block, axis)
        starts = [0] * stacked.ndim
        starts[dim] = place_back(axis, step)
        stacked = lax.dynamic_update_slice(stacked, expand(block), tuple(starts))
    return stacked


FIRST = (1, 3)
SECOND = (3, 1)


def exchange(value, axis, masks):
    names = ("core", "y") if axis == "y" else (axis, "core")
    pairs = []
    for place in range(4):
        for core in range(2):
            target = place ^ masks[core]
            if axis == "y":
                pairs.append((core * 4 + place, core * 4 + target))
            else:
                pairs.append((place * 2 + core, target * 2 + core))
    return lax.ppermute(value, names, pairs)


def spots(axis):
    core = lax.axis_index("core")
    place = lax.axis_index(axis)
    return place, place ^ (3 - 2 * core), place ^ (1 + 2 * core), place ^ 2


def take(blocks, axis, dim):
    return [lax.dynamic_index_in_dim(blocks, spot, dim, keepdims=False) for spot in spots(axis)]


def add(*values):
    total = values[0].astype(F32)
    for value in values[1:]:
        total = total + value.astype(F32)
    return total.astype(BF)


def scatter_start(blocks, axis, dim):
    _, _, first, across = take(blocks, axis, dim)
    return exchange(jnp.stack([first, across]), axis, FIRST)


def scatter_next(blocks, got, axis, dim):
    return add(got[1], take(blocks, axis, dim)[1])


def scatter_end(blocks, got, last, axis, dim):
    return add(got[0], take(blocks, axis, dim)[0], last)


def scatter_ring(blocks, axis, dim):
    got = scatter_start(blocks, axis, dim)
    last = exchange(scatter_next(blocks, got, axis, dim), axis, SECOND)
    return scatter_end(blocks, got, last, axis, dim)


def sum_all(value):
    spread = jnp.broadcast_to(value, (128, 128))
    return jnp.sum(lax.all_to_all(spread, AXES, 0, 0, tiled=True)[:, 0])


def split_cols(shard, groups, width):
    rows = shard.shape[0]
    parts = shard.reshape(rows, groups, 16, 2, width)
    return [parts[:, :, :, core, :].reshape(rows, groups * 16 * width) for core in range(2)]


def join_cols(halves, groups, width):
    rows = halves[0].shape[0]
    parts = [half.reshape(rows, groups, 16, 1, width) for half in halves]
    return jnp.concatenate(parts, axis=3).reshape(rows, groups * 32 * width)


def pick(core, zero, one):
    return jnp.where(core == 0, zero, one)


def delay_rows(values, offset):
    if offset == 0:
        return values
    return jnp.concatenate([jnp.zeros_like(values[:, :offset]), values[:, :-offset]], axis=1)


def advance_rows(values, offset):
    if offset == 0:
        return values
    return jnp.concatenate([values[:, offset:], jnp.zeros_like(values[:, :offset])], axis=1)


def tap_masks(lengths):
    ends = jnp.cumsum(lengths, axis=1)
    starts = ends - lengths
    places = jnp.arange(TOK, dtype=jnp.int32)
    begin = jnp.max(
        jnp.where(starts[:, None, :] <= places[None, :, None], starts[:, None, :], 0), axis=2
    )
    return [(places[None, :] - offset >= begin).astype(F32)[:, :, None] for offset in range(3)]


def adam_step(weight, first, second, grad, rate, decay):
    first = beta_one * first + (1.0 - beta_one) * grad
    second = beta_two * second + (1.0 - beta_two) * grad * grad
    mean_hat = first / (1.0 - beta_one**STEP)
    var_hat = second / (1.0 - beta_two**STEP)
    weight = weight - rate * (mean_hat / (jnp.sqrt(var_hat) + adam_eps) + decay * weight)
    return (weight, first, second)


def gather_weights(core, in_weight, out_weight, ffn_weight, down_weight, conv_weight, gains):
    in_halves = split_cols(in_weight.astype(BF), 3, 32)
    ffn_halves = split_cols(ffn_weight.astype(BF), 2, 144)
    gains_low = jnp.pad(gains.astype(BF), ((0, 6), (0, 120)))
    keep = jnp.concatenate([pick(core, *in_halves), pick(core, *ffn_halves), gains_low], axis=1)
    send = jnp.concatenate(
        [pick(core, *in_halves[::-1]), pick(core, *ffn_halves[::-1]), gains_low], axis=1
    )
    came = swap(send)
    rows = (pick(core, keep, came), pick(core, came, keep))
    small = jnp.concatenate(
        [
            jnp.pad(conv_weight.astype(BF), ((0, 0), (0, 120))),
            rows[0][:2, -128:],
            rows[1][:2, -128:],
            jnp.zeros((1, 128), BF),
        ],
        axis=0,
    )
    in_cols = 3 * CH
    conv = jnp.concatenate(
        [rows[0][:, :in_cols], rows[1][:, :in_cols], out_weight.astype(BF), small], axis=1
    )
    conv = lax.all_gather(conv, ("x", "z", "y"), axis=0, tiled=True).reshape(4, 4, 4, 8, -1)
    in_full = jnp.stack([conv[..., :in_cols], conv[..., in_cols : 2 * in_cols]], axis=2)
    in_full = in_full.reshape(D, in_cols)
    out_full = conv[..., 2 * in_cols : 2 * in_cols + D].reshape(CH, D)
    small = conv[..., 2 * in_cols + D : 2 * in_cols + D + 8].astype(F32)
    taps = small[:, :, :, 0:3].transpose(3, 0, 1, 2, 4).reshape(3, CH)
    gain_full = small[:, :, :, 3:7].reshape(4, 4, 4, 2, 2, 8)
    gain_full = gain_full.transpose(4, 0, 1, 3, 2, 5).reshape(2, D)

    gate, up = [
        jnp.stack([row[:, in_cols + k * HID : in_cols + (k + 1) * HID] for row in rows])
        for k in range(2)
    ]
    whole = (4, 4, 2, 4, 8, HID)
    down = gather_ring(down_weight.astype(BF), "y").reshape(144, D)
    gate = gather_ring(gate, "x")
    up = gather_ring(up, "z")
    down = gather_ring(down, "z")
    gate = gather_ring(gate, "y")
    up = gather_ring(up, "x")
    return in_full, out_full, taps, gain_full, (down, gate, up)


ANY = pl.BlockSpec(memory_space=pl.ANY)
WHOLE = (4, 4, 2, 4, 8, HID)
STACKS = [jax.ShapeDtypeStruct(shape, BF) for shape in ((4, 4, 144, D), WHOLE, WHOLE)]


def blank_stacks():
    return pl.pallas_call(lambda *refs: None, out_specs=[ANY] * 3, out_shape=STACKS)()


def gather_last(blocks, gated, finish):
    axes = ("x", "z", "y")
    dims = (0, 1, 3)
    places = (
        lambda value: value[None],
        lambda value: value.transpose(1, 2, 0, 3, 4)[:, None],
        lambda value: value[:, :, :, None],
    )
    stacked = list(blank_stacks())
    for step in range(4):
        if step:
            blocks = [hop(block, axis) for block, axis in zip(blocks, axes)]
        if step == 2:
            *blocks, gated = lax.optimization_barrier((*blocks, gated))
        if step == 3:
            blocks, beside = lax.optimization_barrier((blocks, finish(gated)))
        for k in range(3):
            starts = [0] * stacked[k].ndim
            starts[dims[k]] = place_back(axes[k], step)
            stacked[k] = lax.dynamic_update_slice(stacked[k], places[k](blocks[k]), tuple(starts))
    down, gate, up = stacked
    return down.reshape(HID, D), gate.reshape(D, HID), up.reshape(D, HID), beside


TILE = 768


def ffn_kernel(
    normed, cot, gate_w, up_w, down_w, grad_down, grad_gate, grad_up, d_normed, out, normed_t
):
    @pl.when(pl.program_id(0) == 0)
    def _():
        normed_t[...] = normed[...].T
        d_normed[...] = jnp.zeros_like(d_normed)
        out[...] = jnp.zeros_like(out)

    gate_pre = dot(normed[...], gate_w[...])
    up_pre = dot(normed[...], up_w[...])
    d_product = dot_nt(cot[...], down_w[...])
    sigmoid_gate = jax.nn.sigmoid(gate_pre)
    silu_gate = gate_pre * sigmoid_gate
    product = (silu_gate * up_pre).astype(BF)
    d_gate = (d_product * up_pre * sigmoid_gate * (1.0 + gate_pre * (1.0 - sigmoid_gate))).astype(BF)
    d_up = (d_product * silu_gate).astype(BF)
    grad_gate[...] = dot(normed_t[...], d_gate).astype(BF)
    grad_up[...] = dot(normed_t[...], d_up).astype(BF)
    grad_down[...] = dot_tn(product, cot[...]).astype(BF)
    d_normed[...] += dot_nt(d_gate, gate_w[...]) + dot_nt(d_up, up_w[...])
    out[...] += dot(product, down_w[...])


def ffn_block(normed, cot, gate_w, up_w, down_w):
    rows = normed.shape[0]
    fixed = lambda shape: pl.BlockSpec(shape, lambda i: (0, 0))
    wide = pl.BlockSpec((D, TILE), lambda i: (0, i))
    tall = pl.BlockSpec((TILE, D), lambda i: (i, 0))
    return pl.pallas_call(
        ffn_kernel,
        grid=(HID // TILE,),
        in_specs=[fixed((rows, D)), fixed((rows, D)), wide, wide, tall],
        out_specs=[tall, wide, wide, fixed((rows, D)), fixed((rows, D))],
        out_shape=[
            jax.ShapeDtypeStruct((HID, D), BF),
            jax.ShapeDtypeStruct((D, HID), BF),
            jax.ShapeDtypeStruct((D, HID), BF),
            jax.ShapeDtypeStruct((rows, D), F32),
            jax.ShapeDtypeStruct((rows, D), F32),
        ],
        scratch_shapes=[pltpu.VMEM((D, rows), BF)],
        compiler_params=pltpu.CompilerParams(
            dimension_semantics=("arbitrary",), vmem_limit_bytes=56 * 1024 * 1024
        ),
        cost_estimate=pl.CostEstimate(
            flops=18 * rows * D * HID, bytes_accessed=40 * 1024 * 1024, transcendentals=rows * HID
        ),
    )(normed, cot, gate_w, up_w, down_w)


def shards(
    tokens,
    doc_lengths,
    cotangent,
    in_weight,
    in_first,
    in_second,
    out_weight,
    out_first,
    out_second,
    ffn_weight,
    ffn_first,
    ffn_second,
    down_weight,
    down_first,
    down_second,
    conv_weight,
    conv_first,
    conv_second,
    gains,
    gains_first,
    gains_second,
):
    core = lax.axis_index("core")
    in_full, out_full, taps, gain_full, blocks = gather_weights(
        core, in_weight, out_weight, ffn_weight, down_weight, conv_weight, gains
    )
    other_tokens = swap(tokens)
    other_cot = swap(cotangent)
    other_lengths = swap(doc_lengths)
    values = jnp.concatenate(
        [pick(core, tokens, other_tokens), pick(core, other_tokens, tokens)], axis=0
    ).astype(F32)
    cot = jnp.concatenate([pick(core, cotangent, other_cot), pick(core, other_cot, cotangent)], axis=0)
    lengths = jnp.concatenate(
        [pick(core, doc_lengths, other_lengths), pick(core, other_lengths, doc_lengths)], axis=0
    )
    masks = tap_masks(lengths)
    gain_one = gain_full[0]
    gain_two = gain_full[1]

    def own_rows(value):
        return lax.dynamic_slice_in_dim(value, core * TOK, TOK, 0)

    def other_rows(value):
        return lax.dynamic_slice_in_dim(value, (1 - core) * TOK, TOK, 0)

    inverse_one = lax.rsqrt(jnp.mean(values * values, axis=1, keepdims=True) + eps_norm)
    normed_one = (values * inverse_one * gain_one).astype(BF)
    projected = dot(normed_one, in_full).reshape(2, TOK, 3 * CH)
    b_part = projected[..., :CH]
    c_part = projected[..., CH : 2 * CH]
    v_part = projected[..., 2 * CH :]
    mixed_in = b_part * v_part
    shifted = [delay_rows(mixed_in, offset) * masks[offset] for offset in range(3)]
    conv_out = taps[0] * shifted[0] + taps[1] * shifted[1] + taps[2] * shifted[2]
    gated = (c_part * conv_out).astype(BF).reshape(2 * TOK, CH)

    def finish(gated):
        branch = dot(gated, out_full)
        middle = values + (branch + swap(branch))
        inverse_two = lax.rsqrt(jnp.mean(middle * middle, axis=1, keepdims=True) + eps_norm)
        return gated, middle, inverse_two, (middle * inverse_two * gain_two).astype(BF)

    down_full, gate_full, up_full, (gated, middle, inverse_two, normed_two) = gather_last(
        blocks, gated, finish
    )
    grad_down, grad_gate, grad_up, d_normed_part, ffn_out = ffn_block(
        normed_two, cot, gate_full, up_full, down_full
    )
    d_normed_two = d_normed_part + swap(d_normed_part)
    grad_gain_two = jnp.sum(d_normed_two * middle * inverse_two, axis=0)
    scaled_two = d_normed_two * gain_two
    d_middle = (
        cot.astype(F32)
        + inverse_two * scaled_two
        - middle * inverse_two**3 * jnp.mean(scaled_two * middle, axis=1, keepdims=True)
    )
    d_middle_low = d_middle.astype(BF)
    grad_out = dot_tn(gated, d_middle_low).astype(BF)
    d_gated = dot_nt(d_middle_low, out_full).reshape(2, TOK, CH)
    d_c_part = d_gated * conv_out
    d_conv = d_gated * c_part
    grad_taps = jnp.stack([jnp.sum(d_conv * shifted[k], axis=(0, 1)) for k in range(3)])
    d_mixed = taps[0] * d_conv
    for offset in (1, 2):
        d_mixed = d_mixed + taps[offset] * advance_rows(d_conv * masks[offset], offset)
    d_proj = (
        jnp.concatenate([d_mixed * v_part, d_c_part, d_mixed * b_part], axis=-1)
        .astype(BF)
        .reshape(2 * TOK, 3 * CH)
    )
    grad_in = dot_tn(normed_one, d_proj).astype(BF)
    in_rows = grad_in.reshape(4, 4, 2, 4, 8, 3 * CH)
    out_rows = grad_out.reshape(4, 4, 4, 8, D)
    conv = jnp.concatenate([in_rows[:, :, 0], in_rows[:, :, 1], out_rows], axis=-1)
    conv = conv.reshape(512, 4096)

    grads = (
        grad_down.reshape(4, 4, 144, D),
        grad_gate.reshape(4, 4, 2, 4, 8, HID),
        grad_up.reshape(4, 4, 2, 4, 8, HID),
    )
    axes = ("x", "z", "y")
    dims = (0, 1, 3)
    got = [scatter_start(*item) for item in zip(grads, axes, dims)]
    summed = lax.psum_scatter(conv, ("x", "z"), scatter_dimension=0, tiled=True)
    *got, _ = lax.optimization_barrier((*got, conv))
    moving = [scatter_next(*item) for item in zip(grads, got, axes, dims)]
    last = [exchange(value, axis, SECOND) for value, axis in zip(moving, axes)]
    *last, ffn_out = lax.optimization_barrier((*last, ffn_out))
    part_a, part_b, part_c = [scatter_end(*item) for item in zip(grads, got, last, axes, dims)]

    d_first_part = dot_nt(d_proj, in_full)
    d_normed_one = own_rows(d_first_part) + swap(other_rows(d_first_part))
    own_values = tokens.astype(F32)
    own_inverse = own_rows(inverse_one)
    grad_gain_one = jnp.sum(d_normed_one * own_values * own_inverse, axis=0)
    scaled_one = d_normed_one * gain_one
    tokens_grad = (
        own_rows(d_middle)
        + own_inverse * scaled_one
        - own_values * own_inverse**3 * jnp.mean(scaled_one * own_values, axis=1, keepdims=True)
    )
    output = (own_rows(middle) + (own_rows(ffn_out) + swap(other_rows(ffn_out)))).astype(BF)

    gain_sums = jnp.stack([grad_gain_one + swap(grad_gain_one), grad_gain_two])
    gain_sums = gain_sums.reshape(2, 16, 2, 32)
    gain_sums = pick(core, gain_sums[:, :, 0], gain_sums[:, :, 1]).reshape(2, CH)
    small = jnp.concatenate([grad_taps, gain_sums, jnp.zeros((3, CH), F32)], axis=0)
    small = small.reshape(8, 64, 8).transpose(1, 0, 2).reshape(64, 64)
    small = lax.all_to_all(small, ("x", "z", "y"), 0, 0, tiled=True)
    part_a, part_b, part_c, small = lax.optimization_barrier((part_a, part_b, part_c, small))
    owned_small = jnp.sum(small, axis=0).reshape(8, 8)
    owned_taps = owned_small[:3]
    owned_gains = owned_small[3:5]

    part_a = scatter_ring(part_a, "z", 0)
    part_b = scatter_ring(part_b, "y", 2)
    part_c = scatter_ring(part_c, "x", 0)
    part_a, part_b, part_c, summed = lax.optimization_barrier((part_a, part_b, part_c, summed))
    owned_down = scatter_ring(part_a.reshape(4, 36, D), "y", 0)
    part_b = scatter_ring(part_b, "x", 0)
    part_c = scatter_ring(part_c, "z", 0)
    conv = scatter_ring(summed.reshape(4, 8, 4096), "y", 0)

    local_squares = F32(0.0)
    for part in (owned_down, part_b, part_c, conv, owned_small[:5]):
        part = part.astype(F32)
        local_squares = local_squares + jnp.sum(part * part)
    squares = sum_all(local_squares)
    grad_norm = jnp.sqrt(squares)
    factor = jnp.minimum(1.0, clip_level / grad_norm)

    def rows_of(which):
        zero, one = [
            jnp.concatenate(
                [
                    conv[:, place * 3 * CH : (place + 1) * 3 * CH],
                    part_b[place],
                    part_c[place],
                ],
                axis=1,
            )
            for place in range(2)
        ]
        return pick(which, zero, one)

    held = rows_of(core)
    came = swap(rows_of(1 - core))
    halves = (pick(core, held, came).astype(F32), pick(core, came, held).astype(F32))
    owned_in = join_cols([half[:, : 3 * CH] for half in halves], 3, 32)
    owned_ffn = join_cols([half[:, 3 * CH :] for half in halves], 2, 144)
    owned_out = conv[:, 6 * CH : 6 * CH + D].astype(F32)
    owned = (owned_in, owned_out, owned_ffn, owned_down.astype(F32), owned_taps, owned_gains)

    *owned, factor = lax.optimization_barrier((*owned, factor))
    states = (
        (in_weight, in_first, in_second),
        (out_weight, out_first, out_second),
        (ffn_weight, ffn_first, ffn_second),
        (down_weight, down_first, down_second),
        (conv_weight, conv_first, conv_second),
        (gains, gains_first, gains_second),
    )
    results = []
    for index in range(6):
        rate = rate_matrix if index < 4 else rate_vector
        decay = decay_matrix if index < 4 else 0.0
        weight, first, second = states[index]
        results.extend(adam_step(weight, first, second, owned[index] * factor, rate, decay))
    return (output, tokens_grad, grad_norm, *results)


def solution(mesh):
    chips = Mesh(mesh.devices.reshape(4, 4, 2, 4), AXES)
    rows = P(AXES, None)
    columns = P(None, AXES)
    return jax.shard_map(
        shards,
        mesh=chips,
        in_specs=(rows,) * 15 + (columns,) * 6,
        out_specs=(rows, rows, P()) + (rows,) * 12 + (columns,) * 6,
        check_vma=False,
    )
```

```python
import jax
import jax.numpy as jnp
from jax import lax
from jax.experimental import pallas as pl
from jax.experimental.pallas import tpu as pltpu
from jax.sharding import Mesh
from jax.sharding import PartitionSpec as P

D = 1024
FF = 4608
STEP = 10
TOK = 256
CH = 512
HID = 2304


eps_norm = 1e-05
beta_one = 0.9
beta_two = 0.95
adam_eps = 1e-08
clip_level = 1.0
rate_matrix = 0.03
rate_vector = 0.5
decay_matrix = 0.1

BF = jnp.bfloat16
F32 = jnp.float32
AXES = ("x", "z", "core", "y")


def dot(left, right):
    return jnp.dot(left, right, preferred_element_type=F32)


def dot_tn(left, right):
    return lax.dot_general(left, right, (((0,), (0,)), ((), ())), preferred_element_type=F32)


def dot_nt(left, right):
    return lax.dot_general(left, right, (((1,), (1,)), ((), ())), preferred_element_type=F32)


def ring_pairs(axis):
    pairs = []
    for place in range(4):
        for core in range(2):
            target = (place + (1 if core == 0 else -1)) % 4
            if axis == "y":
                pairs.append((core * 4 + place, core * 4 + target))
            else:
                pairs.append((place * 2 + core, target * 2 + core))
    return pairs


def hop(value, axis):
    names = ("core", "y") if axis == "y" else (axis, "core")
    return lax.ppermute(value, names, ring_pairs(axis))


def swap(value):
    return lax.ppermute(value, "core", [(0, 1), (1, 0)])


def place_back(axis, steps):
    core = lax.axis_index("core")
    sign = 1 - 2 * core
    return lax.rem(lax.axis_index(axis) - steps * sign + 8, 4)


def gather_ring(block, axis, dest=None, dim=0, expand=None):
    expand = expand or (lambda value: value[None])
    stacked = jnp.zeros(dest or (4,) + block.shape, block.dtype)
    for step in range(4):
        if step:
            block = hop(block, axis)
        starts = [0] * stacked.ndim
        starts[dim] = place_back(axis, step)
        stacked = lax.dynamic_update_slice(stacked, expand(block), tuple(starts))
    return stacked


FIRST = (1, 3)
SECOND = (3, 1)


def exchange(value, axis, masks):
    names = ("core", "y") if axis == "y" else (axis, "core")
    pairs = []
    for place in range(4):
        for core in range(2):
            target = place ^ masks[core]
            if axis == "y":
                pairs.append((core * 4 + place, core * 4 + target))
            else:
                pairs.append((place * 2 + core, target * 2 + core))
    return lax.ppermute(value, names, pairs)


def spots(axis):
    core = lax.axis_index("core")
    place = lax.axis_index(axis)
    return place, place ^ (3 - 2 * core), place ^ (1 + 2 * core), place ^ 2


def take(blocks, axis, dim):
    return [lax.dynamic_index_in_dim(blocks, spot, dim, keepdims=False) for spot in spots(axis)]


def add(*values):
    total = values[0].astype(F32)
    for value in values[1:]:
        total = total + value.astype(F32)
    return total.astype(BF)


def scatter_start(blocks, axis, dim):
    _, _, first, across = take(blocks, axis, dim)
    return exchange(jnp.stack([first, across]), axis, FIRST)


def scatter_next(blocks, got, axis, dim):
    return add(got[1], take(blocks, axis, dim)[1])


def scatter_end(blocks, got, last, axis, dim):
    return add(got[0], take(blocks, axis, dim)[0], last)


def scatter_ring(blocks, axis, dim):
    got = scatter_start(blocks, axis, dim)
    last = exchange(scatter_next(blocks, got, axis, dim), axis, SECOND)
    return scatter_end(blocks, got, last, axis, dim)


def sum_all(value):
    spread = jnp.broadcast_to(value, (128, 128))
    return jnp.sum(lax.all_to_all(spread, AXES, 0, 0, tiled=True)[:, 0])


def split_cols(shard, groups, width):
    rows = shard.shape[0]
    parts = shard.reshape(rows, groups, 16, 2, width)
    return [parts[:, :, :, core, :].reshape(rows, groups * 16 * width) for core in range(2)]


def join_cols(halves, groups, width):
    rows = halves[0].shape[0]
    parts = [half.reshape(rows, groups, 16, 1, width) for half in halves]
    return jnp.concatenate(parts, axis=3).reshape(rows, groups * 32 * width)


def pick(core, zero, one):
    return jnp.where(core == 0, zero, one)


def delay_rows(values, offset):
    if offset == 0:
        return values
    return jnp.concatenate([jnp.zeros_like(values[:, :offset]), values[:, :-offset]], axis=1)


def advance_rows(values, offset):
    if offset == 0:
        return values
    return jnp.concatenate([values[:, offset:], jnp.zeros_like(values[:, :offset])], axis=1)


def tap_masks(lengths):
    ends = jnp.cumsum(lengths, axis=1)
    starts = ends - lengths
    places = jnp.arange(TOK, dtype=jnp.int32)
    begin = jnp.max(
        jnp.where(starts[:, None, :] <= places[None, :, None], starts[:, None, :], 0), axis=2
    )
    return [(places[None, :] - offset >= begin).astype(F32)[:, :, None] for offset in range(3)]


def adam_step(weight, first, second, grad, rate, decay):
    first = beta_one * first + (1.0 - beta_one) * grad
    second = beta_two * second + (1.0 - beta_two) * grad * grad
    mean_hat = first / (1.0 - beta_one**STEP)
    var_hat = second / (1.0 - beta_two**STEP)
    weight = weight - rate * (mean_hat / (jnp.sqrt(var_hat) + adam_eps) + decay * weight)
    return (weight, first, second)


def gather_weights(core, in_weight, out_weight, ffn_weight, down_weight, conv_weight, gains):
    in_halves = split_cols(in_weight.astype(BF), 3, 32)
    ffn_halves = split_cols(ffn_weight.astype(BF), 2, 144)
    gains_low = jnp.pad(gains.astype(BF), ((0, 6), (0, 120)))
    keep = jnp.concatenate([pick(core, *in_halves), pick(core, *ffn_halves), gains_low], axis=1)
    send = jnp.concatenate(
        [pick(core, *in_halves[::-1]), pick(core, *ffn_halves[::-1]), gains_low], axis=1
    )
    came = swap(send)
    rows = (pick(core, keep, came), pick(core, came, keep))
    small = jnp.concatenate(
        [
            jnp.pad(conv_weight.astype(BF), ((0, 0), (0, 120))),
            rows[0][:2, -128:],
            rows[1][:2, -128:],
            jnp.zeros((1, 128), BF),
        ],
        axis=0,
    )
    in_cols = 3 * CH
    conv = jnp.concatenate(
        [rows[0][:, :in_cols], rows[1][:, :in_cols], out_weight.astype(BF), small], axis=1
    )
    conv = lax.all_gather(conv, ("x", "z", "y"), axis=0, tiled=True).reshape(4, 4, 4, 8, -1)
    in_full = jnp.stack([conv[..., :in_cols], conv[..., in_cols : 2 * in_cols]], axis=2)
    in_full = in_full.reshape(D, in_cols)
    out_full = conv[..., 2 * in_cols : 2 * in_cols + D].reshape(CH, D)
    small = conv[..., 2 * in_cols + D : 2 * in_cols + D + 8].astype(F32)
    taps = small[:, :, :, 0:3].transpose(3, 0, 1, 2, 4).reshape(3, CH)
    gain_full = small[:, :, :, 3:7].reshape(4, 4, 4, 2, 2, 8)
    gain_full = gain_full.transpose(4, 0, 1, 3, 2, 5).reshape(2, D)

    gate, up = [
        jnp.stack([row[:, in_cols + k * HID : in_cols + (k + 1) * HID] for row in rows])
        for k in range(2)
    ]
    whole = (4, 4, 2, 4, 8, HID)
    down = gather_ring(down_weight.astype(BF), "y").reshape(144, D)
    gate = gather_ring(gate, "x")
    up = gather_ring(up, "z")
    down = gather_ring(down, "z")
    gate = gather_ring(gate, "y")
    up = gather_ring(up, "x")
    return in_full, out_full, taps, gain_full, (down, gate, up)


ANY = pl.BlockSpec(memory_space=pl.ANY)
WHOLE = (4, 4, 2, 4, 8, HID)
STACKS = [jax.ShapeDtypeStruct(shape, BF) for shape in ((4, 4, 144, D), WHOLE, WHOLE)]


def blank_stacks():
    return pl.pallas_call(lambda *refs: None, out_specs=[ANY] * 3, out_shape=STACKS)()


def gather_last(blocks, gated, finish):
    axes = ("x", "z", "y")
    dims = (0, 1, 3)
    places = (
        lambda value: value[None],
        lambda value: value.transpose(1, 2, 0, 3, 4)[:, None],
        lambda value: value[:, :, :, None],
    )
    stacked = list(blank_stacks())
    for step in range(4):
        if step:
            blocks = [hop(block, axis) for block, axis in zip(blocks, axes)]
        if step == 2:
            *blocks, gated = lax.optimization_barrier((*blocks, gated))
        if step == 3:
            blocks, beside = lax.optimization_barrier((blocks, finish(gated)))
        for k in range(3):
            starts = [0] * stacked[k].ndim
            starts[dims[k]] = place_back(axes[k], step)
            stacked[k] = lax.dynamic_update_slice(stacked[k], places[k](blocks[k]), tuple(starts))
    down, gate, up = stacked
    return down.reshape(HID, D), gate.reshape(D, HID), up.reshape(D, HID), beside


TILE = 768


def ffn_kernel(
    normed, cot, gate_w, up_w, down_w, grad_down, grad_gate, grad_up, d_normed, out, normed_t
):
    @pl.when(pl.program_id(0) == 0)
    def _():
        normed_t[...] = normed[...].T
        d_normed[...] = jnp.zeros_like(d_normed)
        out[...] = jnp.zeros_like(out)

    gate_pre = dot(normed[...], gate_w[...])
    up_pre = dot(normed[...], up_w[...])
    d_product = dot_nt(cot[...], down_w[...])
    sigmoid_gate = jax.nn.sigmoid(gate_pre)
    silu_gate = gate_pre * sigmoid_gate
    product = (silu_gate * up_pre).astype(BF)
    d_gate = (d_product * up_pre * sigmoid_gate * (1.0 + gate_pre * (1.0 - sigmoid_gate))).astype(BF)
    d_up = (d_product * silu_gate).astype(BF)
    grad_gate[...] = dot(normed_t[...], d_gate).astype(BF)
    grad_up[...] = dot(normed_t[...], d_up).astype(BF)
    grad_down[...] = dot_tn(product, cot[...]).astype(BF)
    d_normed[...] += dot_nt(d_gate, gate_w[...]) + dot_nt(d_up, up_w[...])
    out[...] += dot(product, down_w[...])


def ffn_block(normed, cot, gate_w, up_w, down_w):
    rows = normed.shape[0]
    fixed = lambda shape: pl.BlockSpec(shape, lambda i: (0, 0))
    wide = pl.BlockSpec((D, TILE), lambda i: (0, i))
    tall = pl.BlockSpec((TILE, D), lambda i: (i, 0))
    return pl.pallas_call(
        ffn_kernel,
        grid=(HID // TILE,),
        in_specs=[fixed((rows, D)), fixed((rows, D)), wide, wide, tall],
        out_specs=[tall, wide, wide, fixed((rows, D)), fixed((rows, D))],
        out_shape=[
            jax.ShapeDtypeStruct((HID, D), BF),
            jax.ShapeDtypeStruct((D, HID), BF),
            jax.ShapeDtypeStruct((D, HID), BF),
            jax.ShapeDtypeStruct((rows, D), F32),
            jax.ShapeDtypeStruct((rows, D), F32),
        ],
        scratch_shapes=[pltpu.VMEM((D, rows), BF)],
        compiler_params=pltpu.CompilerParams(
            dimension_semantics=("arbitrary",), vmem_limit_bytes=56 * 1024 * 1024
        ),
        cost_estimate=pl.CostEstimate(
            flops=18 * rows * D * HID, bytes_accessed=40 * 1024 * 1024, transcendentals=rows * HID
        ),
    )(normed, cot, gate_w, up_w, down_w)


def shards(
    tokens,
    doc_lengths,
    cotangent,
    in_weight,
    in_first,
    in_second,
    out_weight,
    out_first,
    out_second,
    ffn_weight,
    ffn_first,
    ffn_second,
    down_weight,
    down_first,
    down_second,
    conv_weight,
    conv_first,
    conv_second,
    gains,
    gains_first,
    gains_second,
):
    core = lax.axis_index("core")
    in_full, out_full, taps, gain_full, blocks = gather_weights(
        core, in_weight, out_weight, ffn_weight, down_weight, conv_weight, gains
    )
    other_tokens = swap(tokens)
    other_cot = swap(cotangent)
    other_lengths = swap(doc_lengths)
    values = jnp.concatenate(
        [pick(core, tokens, other_tokens), pick(core, other_tokens, tokens)], axis=0
    ).astype(F32)
    cot = jnp.concatenate([pick(core, cotangent, other_cot), pick(core, other_cot, cotangent)], axis=0)
    lengths = jnp.concatenate(
        [pick(core, doc_lengths, other_lengths), pick(core, other_lengths, doc_lengths)], axis=0
    )
    masks = tap_masks(lengths)
    gain_one = gain_full[0]
    gain_two = gain_full[1]

    def own_rows(value):
        return lax.dynamic_slice_in_dim(value, core * TOK, TOK, 0)

    def other_rows(value):
        return lax.dynamic_slice_in_dim(value, (1 - core) * TOK, TOK, 0)

    inverse_one = lax.rsqrt(jnp.mean(values * values, axis=1, keepdims=True) + eps_norm)
    normed_one = (values * inverse_one * gain_one).astype(BF)
    projected = dot(normed_one, in_full).reshape(2, TOK, 3 * CH)
    b_part = projected[..., :CH]
    c_part = projected[..., CH : 2 * CH]
    v_part = projected[..., 2 * CH :]
    mixed_in = b_part * v_part
    shifted = [delay_rows(mixed_in, offset) * masks[offset] for offset in range(3)]
    conv_out = taps[0] * shifted[0] + taps[1] * shifted[1] + taps[2] * shifted[2]
    gated = (c_part * conv_out).astype(BF).reshape(2 * TOK, CH)

    def finish(gated):
        branch = dot(gated, out_full)
        middle = values + (branch + swap(branch))
        inverse_two = lax.rsqrt(jnp.mean(middle * middle, axis=1, keepdims=True) + eps_norm)
        return gated, middle, inverse_two, (middle * inverse_two * gain_two).astype(BF)

    down_full, gate_full, up_full, (gated, middle, inverse_two, normed_two) = gather_last(
        blocks, gated, finish
    )
    grad_down, grad_gate, grad_up, d_normed_part, ffn_out = ffn_block(
        normed_two, cot, gate_full, up_full, down_full
    )
    d_normed_two = d_normed_part + swap(d_normed_part)
    grad_gain_two = jnp.sum(d_normed_two * middle * inverse_two, axis=0)
    scaled_two = d_normed_two * gain_two
    d_middle = (
        cot.astype(F32)
        + inverse_two * scaled_two
        - middle * inverse_two**3 * jnp.mean(scaled_two * middle, axis=1, keepdims=True)
    )
    d_middle_low = d_middle.astype(BF)
    grad_out = dot_tn(gated, d_middle_low).astype(BF)
    d_gated = dot_nt(d_middle_low, out_full).reshape(2, TOK, CH)
    d_c_part = d_gated * conv_out
    d_conv = d_gated * c_part
    grad_taps = jnp.stack([jnp.sum(d_conv * shifted[k], axis=(0, 1)) for k in range(3)])
    d_mixed = taps[0] * d_conv
    for offset in (1, 2):
        d_mixed = d_mixed + taps[offset] * advance_rows(d_conv * masks[offset], offset)
    d_proj = (
        jnp.concatenate([d_mixed * v_part, d_c_part, d_mixed * b_part], axis=-1)
        .astype(BF)
        .reshape(2 * TOK, 3 * CH)
    )
    grad_in = dot_tn(normed_one, d_proj).astype(BF)
    in_rows = grad_in.reshape(4, 4, 2, 4, 8, 3 * CH)
    out_rows = grad_out.reshape(4, 4, 4, 8, D)
    conv = jnp.concatenate([in_rows[:, :, 0], in_rows[:, :, 1], out_rows], axis=-1)
    conv = conv.reshape(512, 4096)

    grads = (
        grad_down.reshape(4, 4, 144, D),
        grad_gate.reshape(4, 4, 2, 4, 8, HID),
        grad_up.reshape(4, 4, 2, 4, 8, HID),
    )
    axes = ("x", "z", "y")
    dims = (0, 1, 3)
    got = [scatter_start(*item) for item in zip(grads, axes, dims)]
    summed = lax.psum_scatter(conv, ("x", "z"), scatter_dimension=0, tiled=True)
    got[0], _ = lax.optimization_barrier((got[0], conv))
    moving = [scatter_next(*item) for item in zip(grads, got, axes, dims)]
    last = [exchange(value, axis, SECOND) for value, axis in zip(moving, axes)]
    *last, ffn_out = lax.optimization_barrier((*last, ffn_out))
    part_a, part_b, part_c = [scatter_end(*item) for item in zip(grads, got, last, axes, dims)]

    d_first_part = dot_nt(d_proj, in_full)
    d_normed_one = own_rows(d_first_part) + swap(other_rows(d_first_part))
    own_values = tokens.astype(F32)
    own_inverse = own_rows(inverse_one)
    grad_gain_one = jnp.sum(d_normed_one * own_values * own_inverse, axis=0)
    scaled_one = d_normed_one * gain_one
    tokens_grad = (
        own_rows(d_middle)
        + own_inverse * scaled_one
        - own_values * own_inverse**3 * jnp.mean(scaled_one * own_values, axis=1, keepdims=True)
    )
    output = (own_rows(middle) + (own_rows(ffn_out) + swap(other_rows(ffn_out)))).astype(BF)

    gain_sums = jnp.stack([grad_gain_one + swap(grad_gain_one), grad_gain_two])
    gain_sums = gain_sums.reshape(2, 16, 2, 32)
    gain_sums = pick(core, gain_sums[:, :, 0], gain_sums[:, :, 1]).reshape(2, CH)
    small = jnp.concatenate([grad_taps, gain_sums, jnp.zeros((3, CH), F32)], axis=0)
    small = small.reshape(8, 64, 8).transpose(1, 0, 2).reshape(64, 64)
    small = lax.all_to_all(small, ("x", "z", "y"), 0, 0, tiled=True)
    part_a, part_b, part_c, small = lax.optimization_barrier((part_a, part_b, part_c, small))
    owned_small = jnp.sum(small, axis=0).reshape(8, 8)
    owned_taps = owned_small[:3]
    owned_gains = owned_small[3:5]

    part_a = scatter_ring(part_a, "z", 0)
    part_b = scatter_ring(part_b, "y", 2)
    part_c = scatter_ring(part_c, "x", 0)
    part_a, part_b, part_c, summed = lax.optimization_barrier((part_a, part_b, part_c, summed))
    owned_down = scatter_ring(part_a.reshape(4, 36, D), "y", 0)
    part_b = scatter_ring(part_b, "x", 0)
    part_c = scatter_ring(part_c, "z", 0)
    conv = scatter_ring(summed.reshape(4, 8, 4096), "y", 0)

    local_squares = F32(0.0)
    for part in (owned_down, part_b, part_c, conv, owned_small[:5]):
        part = part.astype(F32)
        local_squares = local_squares + jnp.sum(part * part)
    squares = sum_all(local_squares)
    grad_norm = jnp.sqrt(squares)
    factor = jnp.minimum(1.0, clip_level / grad_norm)

    def rows_of(which):
        zero, one = [
            jnp.concatenate(
                [
                    conv[:, place * 3 * CH : (place + 1) * 3 * CH],
                    part_b[place],
                    part_c[place],
                ],
                axis=1,
            )
            for place in range(2)
        ]
        return pick(which, zero, one)

    held = rows_of(core)
    came = swap(rows_of(1 - core))
    halves = (pick(core, held, came).astype(F32), pick(core, came, held).astype(F32))
    owned_in = join_cols([half[:, : 3 * CH] for half in halves], 3, 32)
    owned_ffn = join_cols([half[:, 3 * CH :] for half in halves], 2, 144)
    owned_out = conv[:, 6 * CH : 6 * CH + D].astype(F32)
    owned = (owned_in, owned_out, owned_ffn, owned_down.astype(F32), owned_taps, owned_gains)

    *owned, factor = lax.optimization_barrier((*owned, factor))
    states = (
        (in_weight, in_first, in_second),
        (out_weight, out_first, out_second),
        (ffn_weight, ffn_first, ffn_second),
        (down_weight, down_first, down_second),
        (conv_weight, conv_first, conv_second),
        (gains, gains_first, gains_second),
    )
    results = []
    for index in range(6):
        rate = rate_matrix if index < 4 else rate_vector
        decay = decay_matrix if index < 4 else 0.0
        weight, first, second = states[index]
        results.extend(adam_step(weight, first, second, owned[index] * factor, rate, decay))
    return (output, tokens_grad, grad_norm, *results)


def solution(mesh):
    chips = Mesh(mesh.devices.reshape(4, 4, 2, 4), AXES)
    rows = P(AXES, None)
    columns = P(None, AXES)
    return jax.shard_map(
        shards,
        mesh=chips,
        in_specs=(rows,) * 15 + (columns,) * 6,
        out_specs=(rows, rows, P()) + (rows,) * 12 + (columns,) * 6,
        check_vma=False,
    )
```
